256 devices in a mesh: dp: 4 (over z_lo), seq: 16 (over z_hi, x, core), head: 4 (over y).
Axes of the slice: x: 4, y: 4, z: 8 (z_hi: 2, z_lo: 4; z = z_hi * 4 + z_lo), core: 2. Of those that a mesh axis runs over, the one named last changes fastest.
Arguments:
- queries: bfloat16 [4, 2048, 4096], P('dp', 'seq', 'head'), may hold values from -8 to 8
- keys: bfloat16 [4, 2048, 1024], P('dp', 'seq', 'head'), may hold values from -8 to 8
- values: bfloat16 [4, 2048, 1024], P('dp', 'seq', 'head'), may hold values from -6 to 6
- grad_out: bfloat16 [4, 2048, 4096], P('dp', 'seq', 'head'), may hold values from -6 to 6
- doc_ids: int32 [4, 2048], P('dp', 'seq'), may hold values from 0 to 7, never falling along the last dimension, each value on 1 to 1536 neighbouring positions
- out_weight: bfloat16 [4096, 4096], P('head'), may hold values from -0.09375 to 0.09375
Outputs:
- layer_out: float32 [4, 2048, 4096], P('dp', 'seq', 'head')
- grad_queries: float32 [4, 2048, 4096], P('dp', 'seq', 'head')
- grad_keys: float32 [4, 2048, 1024], P('dp', 'seq', 'head')
- grad_values: float32 [4, 2048, 1024], P('dp', 'seq', 'head')
- weight_grad: float32 [4096, 4096], P('head', 'seq')
The draws below stay inside these ranges and needn't reach their ends.
Inputs may be any that keep to these rules, and one draw needn't show every extreme that they name: `doc_ids`: never falling along a sequence; every number names a document of 1 to 1536 positions, and one document of each sequence has exactly 1536.
All inputs are finite; a program needn't handle non-finite values.
Results may differ from the reference program's by a relative error of at most 0.035.
Values may be sent and summed in bfloat16 or wider, within the bound.
No kernel may reach another device: no remote copies, remote signals or barrier semaphores. Data moves between devices by JAX's collectives and lax.ppermute only.
A program may use at most 128 MiB of HBM per device.

```python
import math
from functools import partial
import jax
import jax.numpy as jnp
import numpy as np
from jax import lax

D = 4096
QUERY_HEADS = 32
KEY_VALUE_HEADS = 8
HEAD_SIZE = 128
SEQUENCE_TOKENS = 2048
PACKED_SEQUENCES = 4
DOCS = 8
MOST = 1536


def draw_queries(key, part):
    key = jax.random.fold_in(key, 3)
    sampled_values = jnp.clip(jax.random.normal(key, (PACKED_SEQUENCES, SEQUENCE_TOKENS, QUERY_HEADS * HEAD_SIZE), jnp.float32), -6.0, 6.0)
    return sampled_values.astype(jnp.bfloat16)


def draw_keys(key, part):
    key = jax.random.fold_in(key, 5)
    sampled_values = jnp.clip(jax.random.normal(key, (PACKED_SEQUENCES, SEQUENCE_TOKENS, KEY_VALUE_HEADS * HEAD_SIZE), jnp.float32), -6.0, 6.0)
    return sampled_values.astype(jnp.bfloat16)


def shard_levels(rng, shape, shards, smallest, top_value):
    gain, own = 1.0, jax.random.fold_in(rng, 6)
    for axis_at, blocks in shards:
        heights = jnp.exp(jax.random.uniform(jax.random.fold_in(own, axis_at), (blocks,), jnp.float32, smallest / len(shards), top_value / len(shards)))
        gain = gain * jnp.repeat(heights, shape[axis_at] // blocks).reshape([-1 if axis == axis_at else 1 for axis in range(len(shape))])
    return gain


def length_profile(number_of, total, limit, slope):
    portions = [(1 << 20) // math.isqrt(standing ** slope) + 1 for standing in range(2, number_of + 1)]
    surplus, counts = total - limit - (number_of - 1), [1] * (number_of - 1)
    while surplus > 0:
        candidates = [i for i in range(number_of - 1) if counts[i] < limit]
        whole, remaining = sum([portions[i] for i in candidates]), surplus
        for i in candidates:
            more = min(limit - counts[i], max(1, remaining * portions[i] // whole), surplus)
            counts[i] = counts[i] + more
            surplus = surplus - more
    return np.array([limit] + counts)


def ragged_sizes(rng, number_of, total, most, lean):
    if number_of == 2:
        one = jax.random.randint(rng, (), max(1, total - most), min(most, total - 1) + 1)
        return jnp.stack([one, total - one])
    tallies = jnp.asarray(length_profile(number_of, total, most, lean), jnp.int32)
    couples = (number_of - 1) // 2
    source_of, receiver = tallies[1:1 + 2 * couples:2], tallies[2:2 + 2 * couples:2]
    slack = jnp.minimum(source_of - 1, most - receiver)
    moved = jax.random.randint(jax.random.fold_in(rng, 1), (couples,), 0, 1 << 20) % (slack + 1)
    tallies = tallies.at[1:1 + 2 * couples:2].set(source_of - moved).at[2:2 + 2 * couples:2].set(receiver + moved)
    return tallies[jax.random.permutation(jax.random.fold_in(rng, 2), number_of)]


def gaussian(rng, shape, width, reach, cuts=(), kind=jnp.bfloat16):
    drawn = jax.random.normal(rng, shape, jnp.float32) * width
    if len(cuts) > 0:
        drawn = shard_levels(rng, shape, cuts, -0.22, 0.18) * drawn
    return jnp.clip(drawn, min=-reach, max=reach).astype(kind)


def setup_inputs(seed: int = 0) -> dict:
    splits = jax.random.split(jax.random.key(seed), 7)
    queries = draw_queries(jax.random.fold_in(splits[6], 71), 0)
    keys = draw_keys(jax.random.fold_in(splits[6], 71), 0)
    values = gaussian(splits[2], (PACKED_SEQUENCES, SEQUENCE_TOKENS, KEY_VALUE_HEADS * HEAD_SIZE), 1.0, 6.0, ((0, 4), (1, 16), (2, 4)))
    grad_out = gaussian(splits[3], (PACKED_SEQUENCES, SEQUENCE_TOKENS, D), 1.0, 6.0, ((0, 4), (1, 16), (2, 4)))
    doc_ids = jax.vmap(lambda own: jnp.searchsorted(jnp.cumsum(ragged_sizes(own, DOCS, SEQUENCE_TOKENS, MOST, 0)), jnp.arange(SEQUENCE_TOKENS), side="right"))(jax.random.split(splits[4], PACKED_SEQUENCES)).reshape((PACKED_SEQUENCES, SEQUENCE_TOKENS)).astype(jnp.int32)
    out_weight = gaussian(splits[5], (QUERY_HEADS * HEAD_SIZE, D), (QUERY_HEADS * HEAD_SIZE) ** -0.5, 0.09375, ((0, 4),))
    return {"queries": queries, "keys": keys, "values": values, "grad_out": grad_out, "doc_ids": doc_ids, "out_weight": out_weight}


def rounded(values):
    return lax.optimization_barrier(values.astype(jnp.bfloat16)).astype(jnp.float32)


def exact(left, right):
    return jnp.dot(left, right, precision=lax.Precision.HIGHEST)


def kv_group(allowed, operands):
    query_matrix, key_matrix, value_matrix, head_gradient = operands
    scale = HEAD_SIZE ** -0.5
    key_float = key_matrix.astype(jnp.float32)
    value_float = value_matrix.astype(jnp.float32)
    heads_list = []
    grad_list = []
    key_gradient = jnp.zeros(key_float.shape, jnp.float32)
    value_gradient = jnp.zeros(value_float.shape, jnp.float32)
    for member in range(query_matrix.shape[1]):
        query_float = query_matrix[:, member].astype(jnp.float32)
        scores = exact(query_float, key_float.T) * scale
        scores = jnp.where(allowed, scores, -jnp.inf)
        top = jnp.max(scores, axis=1, keepdims=True)
        expd = jnp.exp(scores - top)
        total = jnp.sum(expd, axis=1, keepdims=True)
        probs = expd / total
        heads_out = exact(probs, value_float).astype(jnp.bfloat16)
        log_total = top + jnp.log(total)
        back_probs = jnp.where(allowed, jnp.exp(scores - log_total), 0.0)
        weights = rounded(back_probs)
        grad_float = head_gradient[:, member].astype(jnp.float32)
        delta = jnp.sum(grad_float * heads_out.astype(jnp.float32), axis=1, keepdims=True)
        value_gradient = value_gradient + exact(weights.T, grad_float)
        grad_probs = exact(grad_float, value_float.T)
        grad_scores = rounded(scale * back_probs * (grad_probs - delta))
        grad_list.append(exact(grad_scores, key_float))
        key_gradient = key_gradient + exact(grad_scores.T, query_float)
        heads_list.append(heads_out)
    return (jnp.stack(heads_list, axis=1), jnp.stack(grad_list, axis=1),
            key_gradient, value_gradient)


def reference(queries, keys, values, grad_out, doc_ids, out_weight):
    query_group = QUERY_HEADS // KEY_VALUE_HEADS
    positions = jnp.arange(SEQUENCE_TOKENS, dtype=jnp.int32)
    weight_float = out_weight.astype(jnp.float32)
    layer_list = []
    query_grads = []
    key_gradient_rows = []
    value_gradient_rows = []
    weight_sum = jnp.zeros((QUERY_HEADS * HEAD_SIZE, D), jnp.float32)
    for batch_input in range(PACKED_SEQUENCES):
        docs = doc_ids[batch_input]
        allowed = (docs[:, None] == docs[None, :]) & (positions[None, :] <= positions[:, None])
        grad_float = grad_out[batch_input].astype(jnp.float32)
        head_gradient = exact(grad_float, weight_float.T).astype(jnp.bfloat16)
        query_matrix = queries[batch_input].reshape(SEQUENCE_TOKENS, KEY_VALUE_HEADS, query_group, HEAD_SIZE).transpose(1, 0, 2, 3)
        key_matrix = keys[batch_input].reshape(SEQUENCE_TOKENS, KEY_VALUE_HEADS, HEAD_SIZE).transpose(1, 0, 2)
        value_matrix = values[batch_input].reshape(SEQUENCE_TOKENS, KEY_VALUE_HEADS, HEAD_SIZE).transpose(1, 0, 2)
        split_gradient = head_gradient.reshape(SEQUENCE_TOKENS, KEY_VALUE_HEADS, query_group, HEAD_SIZE).transpose(1, 0, 2, 3)
        heads_out, grad_query, key_gradient, value_gradient = lax.map(
            partial(kv_group, allowed), (query_matrix, key_matrix, value_matrix, split_gradient))
        heads_flat = heads_out.transpose(1, 0, 2, 3).reshape(SEQUENCE_TOKENS, QUERY_HEADS * HEAD_SIZE)
        heads_float = heads_flat.astype(jnp.float32)
        layer_list.append(exact(heads_float, weight_float))
        weight_sum = weight_sum + exact(heads_float.T, grad_float)
        query_grads.append(grad_query.transpose(1, 0, 2, 3).reshape(SEQUENCE_TOKENS, QUERY_HEADS * HEAD_SIZE))
        key_gradient_rows.append(key_gradient.transpose(1, 0, 2).reshape(SEQUENCE_TOKENS, KEY_VALUE_HEADS * HEAD_SIZE))
        value_gradient_rows.append(value_gradient.transpose(1, 0, 2).reshape(SEQUENCE_TOKENS, KEY_VALUE_HEADS * HEAD_SIZE))
    return (jnp.stack(layer_list), jnp.stack(query_grads), jnp.stack(key_gradient_rows),
            jnp.stack(value_gradient_rows), weight_sum)
```

```python
import functools

import jax
import jax.numpy as jnp
from jax import lax
from jax.experimental import pallas as pl
from jax.experimental.pallas import tpu as pltpu
from jax.sharding import PartitionSpec as P

HEAD = 128
ROWS = 128
NEG = -1e30
SCALE = HEAD ** -0.5
LOG2E = 1.4426950408889634
F32 = jnp.float32
BF16 = jnp.bfloat16
VMEM_LIMIT = 48 * 1024 * 1024


def seq_perm(move):
    pairs = []
    for s in range(16):
        z, x, c = s // 8, (s // 2) % 4, s % 2
        nz, nx, nc = move(z, x, c)
        pairs.append((s, nz * 8 + nx * 2 + nc))
    return pairs


def core_swap(value):
    return lax.ppermute(value, "seq", seq_perm(lambda z, x, c: (z, x, 1 - c)))


def x_shift(value, by):
    return lax.ppermute(value, "seq", seq_perm(lambda z, x, c: (z, (x + by) % 4, c)))


def z_swap(value):
    return lax.ppermute(value, "seq", seq_perm(lambda z, x, c: (1 - z, x, c)))


def nt(a, b):
    return lax.dot_general(a, b, (((1,), (1,)), ((), ())), preferred_element_type=F32)


def nn(a, b):
    return lax.dot_general(a, b, (((1,), (0,)), ((), ())), preferred_element_type=F32)


def tn(a, b):
    return lax.dot_general(a, b, (((0,), (0,)), ((), ())), preferred_element_type=F32)


def fill(own_ref, pieces, kv_scr, bias_scr):
    own = own_ref[0]
    z, x, c = own // 8, (own // 2) % 4, own % 2
    key_at = lax.broadcasted_iota(jnp.int32, (ROWS, ROWS), 0)
    query_at = lax.broadcasted_iota(jnp.int32, (ROWS, ROWS), 1)
    lag = key_at - query_at
    query_doc = pieces[0][0, ROWS:ROWS + 1, :ROWS].astype(F32)
    for n, piece in enumerate(pieces):
        other, k = n // 4, n % 4
        for part in range(2):
            at = (2 * n + part) * ROWS
            kv_scr[at:at + ROWS, :] = piece[part, :ROWS, :]
            block = ((z + part) % 2) * 8 + ((x + 4 - k) % 4) * 2 + (c + other) % 2
            doc = piece[part, ROWS:ROWS + 8, :ROWS].astype(F32)
            doc = jnp.broadcast_to(doc[:1, :], (ROWS, ROWS)).T
            allowed = (doc == query_doc) & (lag <= (own - block) * ROWS)
            bias_scr[at:at + ROWS, :] = jnp.where(allowed, 0.0, NEG)


def stack_heads(ref, kv):
    return jnp.concatenate(
        [ref[:, (kv * 4 + g) * HEAD:(kv * 4 + g + 1) * HEAD] for g in range(4)], axis=0
    )


def forward_kernel(own_ref, q_ref, *refs):
    pieces, (o_ref, lse_ref, kv_scr, bias_scr, s_scr) = refs[:8], refs[8:]
    fill(own_ref, pieces, kv_scr, bias_scr)
    step = 256
    count = kv_scr.shape[0] // step
    for kv in range(2):
        q = stack_heads(q_ref, kv)

        def scores(i, top):
            rows = pl.ds(pl.multiple_of(i * step, step), step)
            bias = bias_scr[rows, :]
            s = nt(kv_scr[rows, kv * HEAD:(kv + 1) * HEAD], q)
            s = s + jnp.concatenate([bias] * 4, axis=1)
            s_scr[rows, :] = s
            return jnp.maximum(top, jnp.max(s.reshape(step // 8, 8, 512), axis=0))

        top = lax.fori_loop(0, count, scores, jnp.full((8, 512), NEG, F32))
        top = jnp.max(top, axis=0, keepdims=True)

        def values(i, state):
            total, acc = state
            rows = pl.ds(pl.multiple_of(i * step, step), step)
            p = jnp.exp2((s_scr[rows, :] - top) * (SCALE * LOG2E))
            v = kv_scr[rows, 256 + kv * HEAD:256 + (kv + 1) * HEAD]
            total = total + jnp.sum(p.reshape(step // 8, 8, 512), axis=0)
            return total, acc + tn(v, p.astype(BF16))

        total, acc = lax.fori_loop(
            0, count, values, (jnp.zeros((8, 512), F32), jnp.zeros((HEAD, 512), F32))
        )
        total = jnp.sum(total, axis=0, keepdims=True)
        out = (acc / total).T.astype(BF16)
        for g in range(4):
            o_ref[:, (kv * 4 + g) * HEAD:(kv * 4 + g + 1) * HEAD] = out[g * ROWS:(g + 1) * ROWS]
        lse = top * (SCALE * LOG2E) + jnp.log2(total)
        lse_ref[kv * 8:(kv + 1) * 8, :] = jnp.broadcast_to(lse, (8, 512))


def backward_kernel(own_ref, q_ref, d_ref, o_ref, lse_ref, *refs):
    pieces, (dq_ref, own_out, sib_out, kv_scr, bias_scr) = refs[:8], refs[8:]
    fill(own_ref, pieces, kv_scr, bias_scr)
    step = 256
    for kv in range(2):
        q = stack_heads(q_ref, kv)
        d = stack_heads(d_ref, kv)
        o = stack_heads(o_ref, kv)
        lse = lse_ref[kv * 8:kv * 8 + 1, :]
        product = d.astype(F32) * o.astype(F32)
        delta = jnp.sum(product.T, axis=0, keepdims=True)

        def half(out_ref, base):
            def tile(i, acc):
                rows = pl.ds(pl.multiple_of(base + i * step, step), step)
                k = kv_scr[rows, kv * HEAD:(kv + 1) * HEAD]
                v = kv_scr[rows, 256 + kv * HEAD:256 + (kv + 1) * HEAD]
                bias = bias_scr[rows, :]
                s = nt(k, q) * (SCALE * LOG2E) - lse
                p = jnp.exp2(s + jnp.concatenate([bias] * 4, axis=1))
                dp = nt(v, d)
                ds = (p * (dp - delta) * SCALE).astype(BF16)
                out_ref[i, :, kv * HEAD:(kv + 1) * HEAD] = nn(ds, q).astype(BF16)
                out_ref[i, :, 256 + kv * HEAD:256 + (kv + 1) * HEAD] = nn(
                    p.astype(BF16), d
                ).astype(BF16)
                return acc + tn(k, ds)

            return tile

        acc = lax.fori_loop(0, 4, half(own_out, 0), jnp.zeros((HEAD, 512), F32))
        acc = lax.fori_loop(0, 4, half(sib_out, 1024), acc)
        dq = acc.T
        for g in range(4):
            dq_ref[:, (kv * 4 + g) * HEAD:(kv * 4 + g + 1) * HEAD] = dq[g * ROWS:(g + 1) * ROWS]


def weight_kernel(z_ref, *refs):
    heads, grads, (out_ref, h_scr, g_scr) = refs[:8], refs[8:12], refs[12:]
    z = z_ref[0]
    for n in range(8):
        other, k = n // 4, n % 4
        h_scr[n * ROWS:(n + 1) * ROWS, :] = heads[n][...]
        for part in range(2):
            g_scr[part, n * ROWS:(n + 1) * ROWS, :] = grads[k][other, part]

    def piece(k, carry):
        to = (z + k) % 8
        lanes = pl.ds(pl.multiple_of((to % 4) * 256, 256), 256)
        out_ref[k] = tn(h_scr[:, lanes], g_scr[to // 4]).astype(BF16)
        return carry

    lax.fori_loop(0, 8, piece, 0)


SMEM = pl.BlockSpec(memory_space=pltpu.SMEM)
VMEM = pl.BlockSpec(memory_space=pltpu.VMEM)


def call(kernel, inputs, out_shape, scratch, flops, size):
    return pl.pallas_call(
        kernel,
        out_shape=out_shape,
        in_specs=[SMEM] + [VMEM] * (len(inputs) - 1),
        out_specs=jax.tree.map(lambda _: VMEM, out_shape),
        scratch_shapes=scratch,
        compiler_params=pltpu.CompilerParams(vmem_limit_bytes=VMEM_LIMIT),
        cost_estimate=pl.CostEstimate(flops=flops, bytes_accessed=size, transcendentals=0),
    )(*inputs)


def shards(queries, keys, values, grad_out, doc_ids, out_weight):
    rows = queries.shape[1]
    depth = out_weight.shape[0]
    index = lax.axis_index("seq")
    layer = lax.axis_index("dp")
    z, x, c = index // 8, (index // 2) % 4, index % 2
    own = index.astype(jnp.int32).reshape(1)
    height = (z * 4 + layer).astype(jnp.int32).reshape(1)
    shape = jax.ShapeDtypeStruct

    docs = jnp.tile(doc_ids[0].astype(BF16)[None, :], (16, 4))
    message = jnp.concatenate([jnp.concatenate([keys[0], values[0]], axis=1), docs], axis=0)
    base = jnp.stack([message, z_swap(message)])
    mine = [base] + [x_shift(base, k) for k in (1, 2, 3)]
    pieces = mine + [core_swap(piece) for piece in mine]

    full = lax.all_gather(grad_out[0], "head", axis=0)
    head_grad = sum(
        lax.dot_general(
            full[y], out_weight[:, y * 1024:(y + 1) * 1024], (((1,), (1,)), ((), ())),
            preferred_element_type=F32,
        )
        for y in range(4)
    ).astype(BF16)
    split = full.reshape(2, 2, rows, 2, 2, 256)
    keep = lax.dynamic_index_in_dim(split, c, axis=4, keepdims=False)
    give = lax.dynamic_index_in_dim(split, 1 - c, axis=4, keepdims=False)
    both = jnp.stack([keep, core_swap(give)])
    grads = []
    for k in range(4):
        to = (x + k) % 4
        part = lax.dynamic_index_in_dim(both, to // 2, axis=2, keepdims=False)
        part = lax.dynamic_index_in_dim(part, to % 2, axis=3, keepdims=False)
        grads.append(part if k == 0 else x_shift(part, k))

    q = queries[0]
    tokens = 2048
    heads, lse = call(
        forward_kernel,
        [own, q] + pieces,
        (shape((rows, depth), BF16), shape((16, 512), F32)),
        [
            pltpu.VMEM((tokens, 512), BF16),
            pltpu.VMEM((tokens, ROWS), F32),
            pltpu.VMEM((tokens, 512), F32),
        ],
        2 * 2 * 1024 * 2048 * 128,
        4 << 20,
    )

    near = [heads] + [x_shift(heads, k) for k in (1, 2, 3)]
    far = [core_swap(piece) for piece in near]
    products = call(
        weight_kernel,
        [height] + near + far + grads,
        shape((8, 256, 256), BF16),
        [pltpu.VMEM((1024, depth), BF16), pltpu.VMEM((2, 1024, 256), BF16)],
        2 * 1024 * 1024 * 512,
        4 << 20,
    )
    total = products[0].astype(F32)
    for k in range(1, 8):
        pairs = []
        for at in range(8):
            to = (at + k) % 8
            for r in range(8):
                pairs.append(((at % 4) * 16 + (at // 4) * 8 + r, (to % 4) * 16 + (to // 4) * 8 + r))
        total = total + lax.ppermute(products[k], ("dp", "seq"), pairs).astype(F32)
    mine_w = total.astype(BF16)
    weight_grad = jnp.zeros((4, 256, 256), BF16)
    weight_grad = lax.dynamic_update_index_in_dim(weight_grad, mine_w, layer, 0)
    for k in range(1, 4):
        came = lax.ppermute(mine_w, "dp", [(i, (i + k) % 4) for i in range(4)])
        weight_grad = lax.dynamic_update_index_in_dim(weight_grad, came, (layer + 4 - k) % 4, 0)
    weight_grad = weight_grad.reshape(1024, 256).astype(F32)

    terms = jnp.dot(heads, out_weight, preferred_element_type=F32).astype(BF16)
    layer_out = lax.psum_scatter(terms, "head", scatter_dimension=1, tiled=True).astype(F32)

    grad_query, kept, given = call(
        backward_kernel,
        [own, q, head_grad, heads, lse] + pieces,
        (shape((rows, depth), F32), shape((4, 256, 512), BF16), shape((4, 256, 512), BF16)),
        [pltpu.VMEM((tokens, 512), BF16), pltpu.VMEM((tokens, ROWS), F32)],
        5 * 2 * 1024 * 2048 * 128,
        8 << 20,
    )
    summed = (kept.astype(F32) + core_swap(given).astype(F32)).astype(BF16)
    along = summed[0].astype(F32)
    for k in (1, 2, 3):
        along = along + x_shift(summed[k], -k).astype(F32)
    final = along[:ROWS] + z_swap(along[ROWS:].astype(BF16)).astype(F32)
    return (
        layer_out[None],
        grad_query[None],
        final[:, :256][None],
        final[:, 256:][None],
        weight_grad,
    )


def solution(mesh):
    placed = (
        P("dp", "seq", "head"),
        P("dp", "seq", "head"),
        P("dp", "seq", "head"),
        P("dp", "seq", "head"),
        P("dp", "seq"),
        P("head", None),
    )
    return jax.shard_map(
        shards,
        mesh=mesh,
        in_specs=placed,
        out_specs=(
            P("dp", "seq", "head"),
            P("dp", "seq", "head"),
            P("dp", "seq", "head"),
            P("dp", "seq", "head"),
            P("head", "seq"),
        ),
        check_vma=False,
    )
```

```python
import functools

import jax
import jax.numpy as jnp
from jax import lax
from jax.experimental import pallas as pl
from jax.experimental.pallas import tpu as pltpu
from jax.sharding import PartitionSpec as P

HEAD = 128
ROWS = 128
NEG = -1e30
SCALE = HEAD ** -0.5
LOG2E = 1.4426950408889634
F32 = jnp.float32
BF16 = jnp.bfloat16
VMEM_LIMIT = 48 * 1024 * 1024


def seq_perm(move):
    pairs = []
    for s in range(16):
        z, x, c = s // 8, (s // 2) % 4, s % 2
        nz, nx, nc = move(z, x, c)
        pairs.append((s, nz * 8 + nx * 2 + nc))
    return pairs


def core_swap(value):
    return lax.ppermute(value, "seq", seq_perm(lambda z, x, c: (z, x, 1 - c)))


def x_shift(value, by):
    return lax.ppermute(value, "seq", seq_perm(lambda z, x, c: (z, (x + by) % 4, c)))


def z_swap(value):
    return lax.ppermute(value, "seq", seq_perm(lambda z, x, c: (1 - z, x, c)))


def nt(a, b):
    return lax.dot_general(a, b, (((1,), (1,)), ((), ())), preferred_element_type=F32)


def nn(a, b):
    return lax.dot_general(a, b, (((1,), (0,)), ((), ())), preferred_element_type=F32)


def tn(a, b):
    return lax.dot_general(a, b, (((0,), (0,)), ((), ())), preferred_element_type=F32)


def fill(own_ref, pieces, part, kv_scr, bias_scr, base):
    own = own_ref[0]
    z, x, c = own // 8, (own // 2) % 4, own % 2
    key_at = lax.broadcasted_iota(jnp.int32, (ROWS, ROWS), 0)
    query_at = lax.broadcasted_iota(jnp.int32, (ROWS, ROWS), 1)
    lag = key_at - query_at
    query_doc = own_ref_doc(pieces)
    for n, piece in enumerate(pieces[1]):
        other, k = n // 4, n % 4
        at = base + n * ROWS
        kv_scr[at:at + ROWS, :] = piece[:ROWS, :]
        block = ((z + part) % 2) * 8 + ((x + 4 - k) % 4) * 2 + (c + other) % 2
        doc = piece[ROWS:ROWS + 8, :ROWS].astype(F32)
        doc = jnp.broadcast_to(doc[:1, :], (ROWS, ROWS)).T
        allowed = (doc == query_doc) & (lag <= (own - block) * ROWS)
        bias_scr[at:at + ROWS, :] = jnp.where(allowed, 0.0, NEG)


def own_ref_doc(pieces):
    return pieces[0][ROWS:ROWS + 1, :ROWS].astype(F32)


def stack_heads(ref, kv):
    return jnp.concatenate(
        [ref[:, (kv * 4 + g) * HEAD:(kv * 4 + g + 1) * HEAD] for g in range(4)], axis=0
    )


STEP = 256


def attend(kv, q, top, total, acc, kv_scr, bias_scr, s_scr):
    count = kv_scr.shape[0] // STEP

    def scores(i, best):
        rows = pl.ds(pl.multiple_of(i * STEP, STEP), STEP)
        bias = bias_scr[rows, :]
        s = nt(kv_scr[rows, kv * HEAD:(kv + 1) * HEAD], q)
        s = s + jnp.concatenate([bias] * 4, axis=1)
        s_scr[rows, :] = s
        return jnp.maximum(best, jnp.max(s.reshape(STEP // 8, 8, 512), axis=0))

    best = lax.fori_loop(0, count, scores, jnp.broadcast_to(top, (8, 512)))
    best = jnp.max(best, axis=0, keepdims=True)
    factor = jnp.exp2((top - best) * (SCALE * LOG2E))

    def values(i, state):
        sums, acc = state
        rows = pl.ds(pl.multiple_of(i * STEP, STEP), STEP)
        p = jnp.exp2((s_scr[rows, :] - best) * (SCALE * LOG2E))
        v = kv_scr[rows, 256 + kv * HEAD:256 + (kv + 1) * HEAD]
        sums = sums + jnp.sum(p.reshape(STEP // 8, 8, 512), axis=0)
        return sums, acc + tn(v, p.astype(BF16))

    sums, acc = lax.fori_loop(0, count, values, (jnp.zeros((8, 512), F32), acc * factor))
    return best, total * factor + jnp.sum(sums, axis=0, keepdims=True), acc


def near_kernel(own_ref, q_ref, *refs):
    pieces, (acc_ref, top_ref, total_ref, kv_scr, bias_scr, s_scr) = refs[:8], refs[8:]
    fill(own_ref, (pieces[0], pieces), 0, kv_scr, bias_scr, 0)
    for kv in range(2):
        top, total, acc = attend(
            kv, stack_heads(q_ref, kv), jnp.full((1, 512), NEG, F32), jnp.zeros((1, 512), F32),
            jnp.zeros((HEAD, 512), F32), kv_scr, bias_scr, s_scr,
        )
        acc_ref[kv] = acc
        top_ref[kv] = jnp.broadcast_to(top, (8, 512))
        total_ref[kv] = jnp.broadcast_to(total, (8, 512))


def far_kernel(own_ref, q_ref, message_ref, acc_ref, top_ref, total_ref, *refs):
    pieces, (o_ref, lse_ref, kv_scr, bias_scr, s_scr) = refs[:8], refs[8:]
    fill(own_ref, (message_ref, pieces), 1, kv_scr, bias_scr, 0)
    for kv in range(2):
        top, total, acc = attend(
            kv, stack_heads(q_ref, kv), top_ref[kv, :1], total_ref[kv, :1], acc_ref[kv],
            kv_scr, bias_scr, s_scr,
        )
        out = (acc / total).T.astype(BF16)
        for g in range(4):
            o_ref[:, (kv * 4 + g) * HEAD:(kv * 4 + g + 1) * HEAD] = out[g * ROWS:(g + 1) * ROWS]
        lse = top * (SCALE * LOG2E) + jnp.log2(total)
        lse_ref[kv] = jnp.broadcast_to(lse, (8, 512))


def backward_kernel(own_ref, q_ref, d_ref, o_ref, lse_ref, *refs):
    near, far = refs[:8], refs[8:16]
    dq_ref, own_out, sib_out, kv_scr, bias_scr = refs[16:]
    fill(own_ref, (near[0], near), 0, kv_scr, bias_scr, 0)
    fill(own_ref, (near[0], far), 1, kv_scr, bias_scr, 1024)
    for kv in range(2):
        q = stack_heads(q_ref, kv)
        d = stack_heads(d_ref, kv)
        o = stack_heads(o_ref, kv)
        lse = lse_ref[kv, :1, :]
        product = d.astype(F32) * o.astype(F32)
        delta = jnp.sum(product.T, axis=0, keepdims=True)

        def half(out_ref, part, base):
            def tile(i, acc):
                rows = pl.ds(pl.multiple_of(base + i * STEP, STEP), STEP)
                k = kv_scr[rows, kv * HEAD:(kv + 1) * HEAD]
                v = kv_scr[rows, 256 + kv * HEAD:256 + (kv + 1) * HEAD]
                bias = bias_scr[rows, :]
                s = nt(k, q) * (SCALE * LOG2E) - lse
                p = jnp.exp2(s + jnp.concatenate([bias] * 4, axis=1))
                dp = nt(v, d)
                ds = (p * (dp - delta) * SCALE).astype(BF16)
                dk = nn(ds, q).astype(BF16)
                dv = nn(p.astype(BF16), d).astype(BF16)
                for h in range(2):
                    at = slice(h * ROWS, (h + 1) * ROWS)
                    out_ref[2 * i + h, part, :, kv * HEAD:(kv + 1) * HEAD] = dk[at]
                    out_ref[2 * i + h, part, :, 256 + kv * HEAD:256 + (kv + 1) * HEAD] = dv[at]
                return acc + tn(k, ds)

            return tile

        acc = jnp.zeros((HEAD, 512), F32)
        for part in range(2):
            acc = lax.fori_loop(0, 2, half(own_out, part, part * 1024), acc)
            acc = lax.fori_loop(0, 2, half(sib_out, part, part * 1024 + 512), acc)
        dq = acc.T
        for g in range(4):
            dq_ref[:, (kv * 4 + g) * HEAD:(kv * 4 + g + 1) * HEAD] = dq[g * ROWS:(g + 1) * ROWS]


def weight_kernel(z_ref, *refs):
    heads, mine, sibs, (out_ref, h_scr, g_scr) = refs[:8], refs[8:12], refs[12:16], refs[16:]
    z = z_ref[0]
    for n in range(8):
        h_scr[n * ROWS:(n + 1) * ROWS, :] = heads[n][...]
        for part in range(2):
            rows = slice(n * ROWS, (n + 1) * ROWS)
            g_scr[part, rows, :] = mine[n][0, part] if n < 4 else sibs[n - 4][part]

    def piece(k, carry):
        to = (z + k) % 8
        lanes = pl.ds(pl.multiple_of((to % 4) * 256, 256), 256)
        out_ref[k] = tn(h_scr[:, lanes], g_scr[to // 4]).astype(BF16)
        return carry

    lax.fori_loop(0, 8, piece, 0)


def select_kernel(at_ref, g0, g1, g2, g3, o0, o1, o2, o3, scr):
    x, c, y = at_ref[0], at_ref[1], at_ref[2]
    for k, g in enumerate((g0, g1, g2, g3)):
        scr[(y + 4 - k) % 4] = g[...]
    for k, out in enumerate((o0, o1, o2, o3)):
        to = (x + k) % 4
        for rel in range(2):
            lane = ((to % 2) * 2 + (c + rel) % 2) * 256
            for part in range(2):
                out[rel, part] = scr[part * 2 + to // 2, :, pl.ds(pl.multiple_of(lane, 256), 256)]


def weight_copies(y, by, w_ref, w_scr, sems):
    copies = []
    for k in range(4):
        columns = pl.ds(pl.multiple_of(((y + by * k + 4) % 4) * 1024, 1024), 1024)
        copies.append(pltpu.make_async_copy(w_ref.at[:, columns], w_scr.at[k], sems.at[k]))
    for copy in copies:
        copy.start()
    return copies


def grad_heads_kernel(at_ref, g0, g1, g2, g3, w_ref, out_ref, w_scr, sems):
    copies = weight_copies(at_ref[2], -1, w_ref, w_scr, sems)
    acc = jnp.zeros(out_ref.shape, F32)
    for k, g in enumerate((g0, g1, g2, g3)):
        copies[k].wait()
        acc = acc + nt(g[...], w_scr[k])
    out_ref[...] = acc.astype(BF16)


def project_kernel(at_ref, h_ref, w_ref, own_ref, o1, o2, o3, w_scr, sems):
    copies = weight_copies(at_ref[2], 1, w_ref, w_scr, sems)
    h = h_ref[...]
    for k, out in enumerate((own_ref, o1, o2, o3)):
        copies[k].wait()
        out[...] = nn(h, w_scr[k]).astype(out.dtype)


def spread_kernel(at_ref, p0, p1, p2, p3, out_ref):
    for k, p in enumerate((p0, p1, p2, p3)):
        rows = pl.ds(pl.multiple_of(((at_ref[3] + 4 - k) % 4) * 256, 256), 256)
        out_ref[rows, :] = p[...].astype(F32)


SMEM = pl.BlockSpec(memory_space=pltpu.SMEM)
VMEM = pl.BlockSpec(memory_space=pltpu.VMEM)


ANY = pl.BlockSpec(memory_space=pl.ANY)


def call(kernel, inputs, out_shape, scratch, time, anywhere=()):
    specs = [SMEM] + [ANY if n in anywhere else VMEM for n in range(1, len(inputs))]
    return pl.pallas_call(
        kernel,
        out_shape=out_shape,
        in_specs=specs,
        out_specs=jax.tree.map(lambda _: VMEM, out_shape),
        scratch_shapes=scratch,
        compiler_params=pltpu.CompilerParams(vmem_limit_bytes=VMEM_LIMIT),
        cost_estimate=pl.CostEstimate(
            flops=int(time * 1.1e9), bytes_accessed=1 << 20, transcendentals=0
        ),
    )(*inputs)


def y_shift(value, by):
    return lax.ppermute(value, "head", [(i, (i + by) % 4) for i in range(4)])


def z_shift(value, by):
    pairs = []
    for at in range(8):
        to = (at + by) % 8
        for r in range(8):
            pairs.append(((at % 4) * 16 + (at // 4) * 8 + r, (to % 4) * 16 + (to // 4) * 8 + r))
    return lax.ppermute(value, ("dp", "seq"), pairs)


def added(*parts):
    total = parts[0].astype(F32)
    for part in parts[1:]:
        total = total + part.astype(F32)
    return total


def shards(queries, keys, values, grad_out, doc_ids, out_weight):
    rows = queries.shape[1]
    depth = out_weight.shape[0]
    index = lax.axis_index("seq")
    layer = lax.axis_index("dp")
    y = lax.axis_index("head")
    z, x, c = index // 8, (index // 2) % 4, index % 2
    own = index.astype(jnp.int32).reshape(1)
    height = (z * 4 + layer).astype(jnp.int32).reshape(1)
    place = jnp.stack([x, c, y, layer]).astype(jnp.int32)
    shape = jax.ShapeDtypeStruct

    docs = jnp.tile(doc_ids[0].astype(BF16)[None, :], (16, 4))
    message = jnp.concatenate([jnp.concatenate([keys[0], values[0]], axis=1), docs], axis=0)
    across = z_swap(message)
    near = [message] + [x_shift(message, k) for k in (1, 3, 2)]
    near = [near[0], near[1], near[3], near[2]]
    near = near + [core_swap(piece) for piece in near]
    far = [across] + [x_shift(across, k) for k in (1, 3, 2)]
    far = [far[0], far[1], far[3], far[2]]
    far = far + [core_swap(piece) for piece in far]

    cotangents = [grad_out[0]] + [y_shift(grad_out[0], k) for k in (1, 2, 3)]
    w_scratch = [pltpu.VMEM((4, 1024, 1024), BF16), pltpu.SemaphoreType.DMA((4,))]
    head_grad = call(
        grad_heads_kernel, [place] + cotangents + [out_weight], shape((rows, depth), BF16),
        w_scratch, 6, (5,),
    )
    chosen = call(
        select_kernel, [place] + cotangents, (shape((2, 2, rows, 256), BF16),) * 4,
        [pltpu.VMEM((4, rows, 1024), BF16)], 1.5,
    )
    grads = [chosen[0]] + [x_shift(chosen[k], k) for k in (1, 2, 3)]
    grads_sib = [core_swap(piece[1]) for piece in grads]

    q = queries[0]
    half_scratch = [
        pltpu.VMEM((1024, 512), BF16), pltpu.VMEM((1024, ROWS), F32), pltpu.VMEM((1024, 512), F32)
    ]
    acc, top, total = call(
        near_kernel, [own, q] + near,
        (shape((2, HEAD, 512), F32), shape((2, 8, 512), F32), shape((2, 8, 512), F32)),
        half_scratch, 4,
    )
    heads, lse = call(
        far_kernel, [own, q, message, acc, top, total] + far,
        (shape((rows, depth), BF16), shape((2, 8, 512), F32)), half_scratch, 4,
    )

    close = [heads] + [x_shift(heads, k) for k in (1, 2, 3)]
    sibling = [core_swap(piece) for piece in close]

    grad_query, kept, given = call(
        backward_kernel,
        [own, q, head_grad, heads, lse] + near + far,
        (shape((rows, depth), F32), shape((4, 2, rows, 512), BF16), shape((4, 2, rows, 512), BF16)),
        [pltpu.VMEM((2048, 512), BF16), pltpu.VMEM((2048, ROWS), F32)], 11,
    )

    products = call(
        weight_kernel,
        [height] + close + sibling + grads + grads_sib,
        shape((8, 256, 256), BF16),
        [pltpu.VMEM((1024, depth), BF16), pltpu.VMEM((2, 1024, 256), BF16)], 4,
    )
    up, down = products[4], products[5]
    for k in range(3):
        up = added(z_shift(up, 1), products[3 - k]).astype(BF16)
        down = z_shift(down, -1)
        if k < 2:
            down = added(down, products[6 + k]).astype(BF16)
    block = added(z_shift(up, 1), down, products[0]).astype(BF16)
    blocks = [block] + [
        lax.ppermute(block, "dp", [(i, (i + k) % 4) for i in range(4)]) for k in (1, 2, 3)
    ]
    weight_grad = call(spread_kernel, [place] + blocks, shape((1024, 256), F32), [], 1)

    heads_late, _ = lax.optimization_barrier((heads, products))
    terms = call(
        project_kernel, [place, heads_late, out_weight],
        (shape((rows, 1024), F32),) + (shape((rows, 1024), BF16),) * 3, w_scratch, 6, (2,),
    )
    layer_out = added(terms[0], *[y_shift(terms[k], k) for k in (1, 2, 3)])

    summed = added(kept, core_swap(given)).astype(BF16)
    along = added(summed[0], *[x_shift(summed[k], -k) for k in (1, 2, 3)])
    final = along[0] + z_swap(along[1].astype(BF16)).astype(F32)
    return (
        layer_out[None],
        grad_query[None],
        final[:, :256][None],
        final[:, 256:][None],
        weight_grad,
    )


def solution(mesh):
    placed = (
        P("dp", "seq", "head"),
        P("dp", "seq", "head"),
        P("dp", "seq", "head"),
        P("dp", "seq", "head"),
        P("dp", "seq"),
        P("head", None),
    )
    return jax.shard_map(
        shards,
        mesh=mesh,
        in_specs=placed,
        out_specs=(
            P("dp", "seq", "head"),
            P("dp", "seq", "head"),
            P("dp", "seq", "head"),
            P("dp", "seq", "head"),
            P("head", "seq"),
        ),
        check_vma=False,
    )
```

```python
import functools

import jax
import jax.numpy as jnp
from jax import lax
from jax.experimental import pallas as pl
from jax.experimental.pallas import tpu as pltpu
from jax.sharding import PartitionSpec as P

HEAD = 128
ROWS = 128
NEG = -1e30
SCALE = HEAD ** -0.5
LOG2E = 1.4426950408889634
F32 = jnp.float32
BF16 = jnp.bfloat16
VMEM_LIMIT = 48 * 1024 * 1024


def seq_perm(move):
    pairs = []
    for s in range(16):
        z, x, c = s // 8, (s // 2) % 4, s % 2
        nz, nx, nc = move(z, x, c)
        pairs.append((s, nz * 8 + nx * 2 + nc))
    return pairs


def core_swap(value):
    return lax.ppermute(value, "seq", seq_perm(lambda z, x, c: (z, x, 1 - c)))


def x_swap(value, bits):
    return lax.ppermute(value, "seq", seq_perm(lambda z, x, c: (z, x ^ bits, c)))


def z_swap(value):
    return lax.ppermute(value, "seq", seq_perm(lambda z, x, c: (1 - z, x, c)))


def nt(a, b):
    return lax.dot_general(a, b, (((1,), (1,)), ((), ())), preferred_element_type=F32)


def nn(a, b):
    return lax.dot_general(a, b, (((1,), (0,)), ((), ())), preferred_element_type=F32)


def tn(a, b):
    return lax.dot_general(a, b, (((0,), (0,)), ((), ())), preferred_element_type=F32)


def message_kernel(doc_ref, k_ref, v_ref, out_ref):
    out_ref[:ROWS, :256] = k_ref[...]
    out_ref[:ROWS, 256:] = v_ref[...]
    docs = jnp.broadcast_to(doc_ref[...].astype(F32), (16, ROWS)).astype(BF16)
    for n in range(4):
        out_ref[ROWS:, n * ROWS:(n + 1) * ROWS] = docs


def fill(own_ref, pieces, kv_scr, bias_scr):
    own = own_ref[0]
    z, x, c = own // 8, (own // 2) % 4, own % 2
    key_at = lax.broadcasted_iota(jnp.int32, (ROWS, ROWS), 0)
    query_at = lax.broadcasted_iota(jnp.int32, (ROWS, ROWS), 1)
    lag = key_at - query_at
    query_doc = pieces[0][ROWS:ROWS + 1, :ROWS].astype(F32)
    for n, piece in enumerate(pieces):
        other, part, k = n // 8, (n // 4) % 2, n % 4
        at = n * ROWS
        kv_scr[at:at + ROWS, :] = piece[:ROWS, :]
        block = ((z + part) % 2) * 8 + (x ^ k) * 2 + (c + other) % 2
        doc = piece[ROWS:ROWS + 8, :ROWS].astype(F32)
        doc = jnp.broadcast_to(doc[:1, :], (ROWS, ROWS)).T
        allowed = (doc == query_doc) & (lag <= (own - block) * ROWS)
        bias_scr[at:at + ROWS, :] = jnp.where(allowed, 0.0, NEG)


def each(refs):
    return [ref.at[k] for ref in refs for k in range(ref.shape[0])]


def stack_heads(ref, kv):
    return jnp.concatenate(
        [ref[:, (kv * 4 + g) * HEAD:(kv * 4 + g + 1) * HEAD] for g in range(4)], axis=0
    )


STEP = 256


def attend(kv, q, top, total, acc, kv_scr, bias_scr, s_scr):
    count = kv_scr.shape[0] // STEP

    def scores(i, best):
        rows = pl.ds(pl.multiple_of(i * STEP, STEP), STEP)
        bias = bias_scr[rows, :]
        s = nt(kv_scr[rows, kv * HEAD:(kv + 1) * HEAD], q)
        s = s + jnp.concatenate([bias] * 4, axis=1)
        s_scr[rows, :] = s
        return jnp.maximum(best, jnp.max(s.reshape(STEP // 8, 8, 512), axis=0))

    best = lax.fori_loop(0, count, scores, jnp.broadcast_to(top, (8, 512)), unroll=True)
    best = jnp.max(best, axis=0, keepdims=True)
    factor = jnp.exp2((top - best) * (SCALE * LOG2E))

    def values(i, state):
        sums, acc = state
        rows = pl.ds(pl.multiple_of(i * STEP, STEP), STEP)
        p = jnp.exp2((s_scr[rows, :] - best) * (SCALE * LOG2E))
        v = kv_scr[rows, 256 + kv * HEAD:256 + (kv + 1) * HEAD]
        sums = sums + jnp.sum(p.reshape(STEP // 8, 8, 512), axis=0)
        return sums, acc + tn(v, p.astype(BF16))

    sums, acc = lax.fori_loop(0, count, values, (jnp.zeros((8, 512), F32), acc * factor), unroll=True)
    return best, total * factor + jnp.sum(sums, axis=0, keepdims=True), acc


def forward_kernel(own_ref, q_ref, *refs):
    pieces, (o_ref, lse_ref, kv_scr, bias_scr, s_scr) = each(refs[:2]), refs[2:]
    fill(own_ref, pieces, kv_scr, bias_scr)
    for kv in range(2):
        top, total, acc = attend(
            kv, stack_heads(q_ref, kv), jnp.full((1, 512), NEG, F32), jnp.zeros((1, 512), F32),
            jnp.zeros((HEAD, 512), F32), kv_scr, bias_scr, s_scr,
        )
        out = (acc / total).T.astype(BF16)
        for g in range(4):
            o_ref[:, (kv * 4 + g) * HEAD:(kv * 4 + g + 1) * HEAD] = out[g * ROWS:(g + 1) * ROWS]
        lse = top * (SCALE * LOG2E) + jnp.log2(total)
        lse_ref[kv] = jnp.broadcast_to(lse, (8, 512))


def backward_kernel(own_ref, q_ref, d_ref, o_ref, lse_ref, *refs):
    dq_ref, own_out, sib_out, kv_scr, bias_scr = refs[2:]
    fill(own_ref, each(refs[:2]), kv_scr, bias_scr)
    for kv in range(2):
        q = stack_heads(q_ref, kv)
        d = stack_heads(d_ref, kv)
        o = stack_heads(o_ref, kv)
        lse = lse_ref[kv, :1, :]
        product = d.astype(F32) * o.astype(F32)
        delta = jnp.sum(product.T, axis=0, keepdims=True)

        def half(out_ref, part, base):
            def tile(i, acc):
                rows = pl.ds(pl.multiple_of(base + i * STEP, STEP), STEP)
                k = kv_scr[rows, kv * HEAD:(kv + 1) * HEAD]
                v = kv_scr[rows, 256 + kv * HEAD:256 + (kv + 1) * HEAD]
                bias = bias_scr[rows, :]
                s = nt(k, q) * (SCALE * LOG2E) - lse
                p = jnp.exp2(s + jnp.concatenate([bias] * 4, axis=1))
                dp = nt(v, d)
                ds = (p * (dp - delta) * SCALE).astype(BF16)
                dk = nn(ds, q).astype(BF16)
                dv = nn(p.astype(BF16), d).astype(BF16)
                for h in range(2):
                    at = slice(h * ROWS, (h + 1) * ROWS)
                    out_ref[2 * i + h, part, :, kv * HEAD:(kv + 1) * HEAD] = dk[at]
                    out_ref[2 * i + h, part, :, 256 + kv * HEAD:256 + (kv + 1) * HEAD] = dv[at]
                return acc + tn(k, ds)

            return tile

        acc = jnp.zeros((HEAD, 512), F32)
        for part in range(2):
            acc = lax.fori_loop(0, 2, half(own_out, part, part * 512), acc, unroll=True)
            acc = lax.fori_loop(0, 2, half(sib_out, part, part * 512 + 1024), acc, unroll=True)
        dq = acc.T
        for g in range(4):
            dq_ref[:, (kv * 4 + g) * HEAD:(kv * 4 + g + 1) * HEAD] = dq[g * ROWS:(g + 1) * ROWS]


def weight_kernel(rel, z_ref, *refs):
    heads, grads, (out_ref, h_scr, g_scr) = refs[:4], refs[4:8], refs[8:]
    z = z_ref[0]
    for n in range(4):
        rows = slice(n * ROWS, (n + 1) * ROWS)
        h_scr[rows, :] = heads[n][...]
        for part in range(2):
            g_scr[part, rows, :] = grads[n][rel, part]

    def piece(k, carry):
        to = (z + k) % 8
        lanes = pl.ds(pl.multiple_of((to % 4) * 256, 256), 256)
        out_ref[k] = tn(h_scr[:, lanes], g_scr[to // 4]).astype(BF16)
        return carry

    lax.fori_loop(0, 8, piece, 0, unroll=True)


def select_kernel(at_ref, g0, g1, g2, g3, o0, o1, o2, o3, scr):
    x, c, y = at_ref[0], at_ref[1], at_ref[2]
    for k, g in enumerate((g0, g1, g2, g3)):
        scr[y ^ k] = g[...]
    for k, out in enumerate((o0, o1, o2, o3)):
        to = x ^ k
        for rel in range(2):
            lane = ((to % 2) * 2 + (c + rel) % 2) * 256
            for part in range(2):
                out[rel, part] = scr[part * 2 + to // 2, :, pl.ds(pl.multiple_of(lane, 256), 256)]


def weight_copies(places, w_ref, w_scr, sems):
    copies = []
    for k, place in enumerate(places):
        columns = pl.ds(pl.multiple_of(place * 1024, 1024), 1024)
        copies.append(pltpu.make_async_copy(w_ref.at[:, columns], w_scr.at[k], sems.at[k]))
    for copy in copies:
        copy.start()
    return copies


def grad_heads_kernel(at_ref, g0, g1, g2, g3, w_ref, out_ref, w_scr, sems):
    copies = weight_copies([at_ref[2] ^ k for k in range(4)], w_ref, w_scr, sems)
    acc = jnp.zeros(out_ref.shape, F32)
    for k, g in enumerate((g0, g1, g2, g3)):
        copies[k].wait()
        acc = acc + nt(g[...], w_scr[k])
    out_ref[...] = acc.astype(BF16)


def project_kernel(at_ref, h_ref, w_ref, own_ref, far_ref, w_scr, sems):
    y = at_ref[2]
    copies = weight_copies([y ^ bits for bits in (3, 2, 0, 1)], w_ref, w_scr, sems)
    h = h_ref[...]
    for k in range(4):
        copies[k].wait()
        out = far_ref if k < 2 else own_ref
        out[k % 2] = nn(h, w_scr[k]).astype(out.dtype)


def spread_kernel(at_ref, p0, p1, p2, p3, out_ref):
    for k, p in enumerate((p0, p1, p2, p3)):
        rows = pl.ds(pl.multiple_of((at_ref[3] ^ k) * 256, 256), 256)
        out_ref[rows, :] = p[...].astype(F32)


SMEM = pl.BlockSpec(memory_space=pltpu.SMEM)
VMEM = pl.BlockSpec(memory_space=pltpu.VMEM)


ANY = pl.BlockSpec(memory_space=pl.ANY)


def call(kernel, inputs, out_shape, scratch, time, anywhere=(), first=SMEM):
    specs = [first] + [ANY if n in anywhere else VMEM for n in range(1, len(inputs))]
    return pl.pallas_call(
        kernel,
        out_shape=out_shape,
        in_specs=specs,
        out_specs=jax.tree.map(lambda _: VMEM, out_shape),
        scratch_shapes=scratch,
        compiler_params=pltpu.CompilerParams(vmem_limit_bytes=VMEM_LIMIT),
        cost_estimate=pl.CostEstimate(
            flops=int(time * 6e9), bytes_accessed=1 << 20, transcendentals=0
        ),
    )(*inputs)


def y_swap(value, bits):
    return lax.ppermute(value, "head", [(i, i ^ bits) for i in range(4)])


def z_shift(value, by):
    pairs = []
    for at in range(8):
        to = (at + by) % 8
        for r in range(8):
            pairs.append(((at % 4) * 16 + (at // 4) * 8 + r, (to % 4) * 16 + (to // 4) * 8 + r))
    return lax.ppermute(value, ("dp", "seq"), pairs)


def together(*values):
    return lax.optimization_barrier(values)


def after(value, *others):
    return lax.optimization_barrier((value, *others))[0]


def added(*parts):
    total = parts[0].astype(F32)
    for part in parts[1:]:
        total = total + part.astype(F32)
    return total


def shards(queries, keys, values, grad_out, doc_ids, out_weight):
    rows = queries.shape[1]
    depth = out_weight.shape[0]
    index = lax.axis_index("seq")
    layer = lax.axis_index("dp")
    y = lax.axis_index("head")
    z, x, c = index // 8, (index // 2) % 4, index % 2
    own = index.astype(jnp.int32).reshape(1)
    height = (z * 4 + layer).astype(jnp.int32).reshape(1)
    place = jnp.stack([x, c, y, layer]).astype(jnp.int32)
    shape = jax.ShapeDtypeStruct

    message = call(
        message_kernel, [doc_ids, keys[0], values[0]], shape((rows + 16, 512), BF16), [], 0.5, (),
        VMEM,
    )
    q = queries[0]
    w_scratch = [pltpu.VMEM((4, 1024, 1024), BF16), pltpu.SemaphoreType.DMA((4,))]
    cotangent = after(grad_out[0], message)
    *crossed, across, near1 = together(
        *[y_swap(cotangent, k) for k in (1, 3, 2)], z_swap(message), x_swap(message, 1)
    )
    cotangents = [grad_out[0], crossed[0], crossed[2], crossed[1]]

    chosen = call(
        select_kernel, [place] + cotangents, (shape((2, 2, rows, 256), BF16),) * 4,
        [pltpu.VMEM((4, rows, 1024), BF16)], 1.5,
    )
    head_grad = call(
        grad_heads_kernel, [place] + cotangents + [out_weight], shape((rows, depth), BF16),
        w_scratch, 6, (5,),
    )
    near3, near2, far1, far3, far2, head_grad, *chosen = together(
        x_swap(message, 3), x_swap(message, 2), *[x_swap(across, k) for k in (1, 3, 2)],
        head_grad, *chosen,
    )

    pieces = jnp.stack([message, near1, near2, near3, across, far1, far2, far3])
    theirs, *chosen = together(core_swap(pieces), *chosen)
    pieces = [pieces, theirs]
    heads, lse = call(
        forward_kernel, [own, q] + pieces,
        (shape((rows, depth), BF16), shape((2, 8, 512), F32)),
        [
            pltpu.VMEM((2048, 512), BF16),
            pltpu.VMEM((2048, ROWS), F32),
            pltpu.VMEM((2048, 512), F32),
        ],
        4,
    )
    terms = call(
        project_kernel, [place, heads, out_weight],
        (shape((2, rows, 1024), F32), shape((2, rows, 1024), BF16)), w_scratch, 5, (2,),
    )
    heads, own_terms, far_terms, *grads = together(
        heads, *terms, *[x_swap(chosen[k], k) for k in (3, 2, 1)]
    )
    grads = [chosen[0]] + grads[::-1]

    grad_query, kept, given = call(
        backward_kernel, [own, q, head_grad, heads, lse] + pieces,
        (shape((rows, depth), F32), shape((4, 2, rows, 512), BF16), shape((4, 2, rows, 512), BF16)),
        [pltpu.VMEM((2048, 512), BF16), pltpu.VMEM((2048, ROWS), F32)], 11,
    )
    kept, given, far_terms, *close = together(
        kept, given, far_terms, *[x_swap(heads, k) for k in (1, 2, 3)]
    )
    far_terms = y_swap(far_terms, 3)
    close = [heads] + close

    def products(rel):
        return call(
            functools.partial(weight_kernel, rel), [height] + close + grads,
            shape((8, 256, 256), BF16),
            [pltpu.VMEM((512, depth), BF16), pltpu.VMEM((2, 512, 256), BF16)], 1,
        )

    summed = added(kept, core_swap(given)).astype(BF16)
    theirs = core_swap(products(1))
    ours, theirs, summed = together(products(0), theirs, summed)

    up, down = added(ours[4], theirs[4]).astype(BF16), added(ours[5], theirs[5]).astype(BF16)
    along = summed[0].astype(F32)
    for k in range(3):
        up = added(z_shift(up, 1), ours[3 - k], theirs[3 - k]).astype(BF16)
        down = z_shift(down, -1)
        if k < 2:
            down = added(down, ours[6 + k], theirs[6 + k]).astype(BF16)
        back = x_swap(summed[(1, 3, 2)[k]], (1, 3, 2)[k])
        if k == 0:
            up, down, back, far_terms = together(up, down, back, far_terms)
            halves = own_terms + far_terms.astype(F32)
            far_terms = y_swap(halves[1].astype(BF16), 1)
        if k == 1:
            up, down, back = together(up, down, back)
        if k == 2:
            up, down, back, far_terms = together(up, down, back, far_terms)
            layer_out = halves[0] + far_terms.astype(F32)
        along = along + back.astype(F32)
    block = added(z_shift(up, 1), down, ours[0], theirs[0]).astype(BF16)
    block, layer_out, far_keys = together(block, layer_out, z_swap(along[1].astype(BF16)))

    blocks = [lax.ppermute(block, "dp", [(i, i ^ k) for i in range(4)]) for k in (3, 2, 1)]
    blocks = [block] + blocks[::-1]
    final = along[0] + far_keys.astype(F32)
    weight_grad = call(spread_kernel, [place] + blocks, shape((1024, 256), F32), [], 1)
    return (
        layer_out[None],
        grad_query[None],
        final[:, :256][None],
        final[:, 256:][None],
        weight_grad,
    )


def solution(mesh):
    placed = (
        P("dp", "seq", "head"),
        P("dp", "seq", "head"),
        P("dp", "seq", "head"),
        P("dp", "seq", "head"),
        P("dp", "seq"),
        P("head", None),
    )
    return jax.shard_map(
        shards,
        mesh=mesh,
        in_specs=placed,
        out_specs=(
            P("dp", "seq", "head"),
            P("dp", "seq", "head"),
            P("dp", "seq", "head"),
            P("dp", "seq", "head"),
            P("head", "seq"),
        ),
        check_vma=False,
    )
```

```python
import functools

import jax
import jax.numpy as jnp
from jax import lax
from jax.experimental import pallas as pl
from jax.experimental.pallas import tpu as pltpu
from jax.sharding import PartitionSpec as P

HEAD = 128
ROWS = 128
NEG = -1e30
SCALE = HEAD ** -0.5
LOG2E = 1.4426950408889634
F32 = jnp.float32
BF16 = jnp.bfloat16
VMEM_LIMIT = 48 * 1024 * 1024


def seq_perm(move):
    pairs = []
    for s in range(16):
        z, x, c = s // 8, (s // 2) % 4, s % 2
        nz, nx, nc = move(z, x, c)
        pairs.append((s, nz * 8 + nx * 2 + nc))
    return pairs


def core_swap(value):
    return lax.ppermute(value, "seq", seq_perm(lambda z, x, c: (z, x, 1 - c)))


def x_swap(value, bits):
    return lax.ppermute(value, "seq", seq_perm(lambda z, x, c: (z, x ^ bits, c)))


def z_swap(value):
    return lax.ppermute(value, "seq", seq_perm(lambda z, x, c: (1 - z, x, c)))


def nt(a, b):
    return lax.dot_general(a, b, (((1,), (1,)), ((), ())), preferred_element_type=F32)


def nn(a, b):
    return lax.dot_general(a, b, (((1,), (0,)), ((), ())), preferred_element_type=F32)


def tn(a, b):
    return lax.dot_general(a, b, (((0,), (0,)), ((), ())), preferred_element_type=F32)


def message_kernel(doc_ref, k_ref, v_ref, out_ref, doc_scr, sems):
    copies = [
        pltpu.make_async_copy(doc_ref, doc_scr, sems.at[0]),
        pltpu.make_async_copy(k_ref, out_ref.at[:ROWS, :256], sems.at[1]),
        pltpu.make_async_copy(v_ref, out_ref.at[:ROWS, 256:], sems.at[2]),
    ]
    for copy in copies:
        copy.start()
    copies[0].wait()
    docs = jnp.broadcast_to(doc_scr[...].astype(F32), (16, ROWS)).astype(BF16)
    for n in range(4):
        out_ref[ROWS:, n * ROWS:(n + 1) * ROWS] = docs
    copies[1].wait()
    copies[2].wait()


def fill(own_ref, pieces, kv_scr, bias_scr):
    own = own_ref[0]
    z, x, c = own // 8, (own // 2) % 4, own % 2
    key_at = lax.broadcasted_iota(jnp.int32, (ROWS, ROWS), 0)
    query_at = lax.broadcasted_iota(jnp.int32, (ROWS, ROWS), 1)
    lag = key_at - query_at
    query_doc = pieces[0][ROWS:ROWS + 1, :ROWS].astype(F32)
    for n, piece in enumerate(pieces):
        other, part, k = n // 8, (n // 4) % 2, n % 4
        at = n * ROWS
        kv_scr[at:at + ROWS, :] = piece[:ROWS, :]
        block = ((z + part) % 2) * 8 + (x ^ k) * 2 + (c + other) % 2
        doc = piece[ROWS:ROWS + 8, :ROWS].astype(F32)
        doc = jnp.broadcast_to(doc[:1, :], (ROWS, ROWS)).T
        allowed = (doc == query_doc) & (lag <= (own - block) * ROWS)
        bias_scr[at:at + ROWS, :] = jnp.where(allowed, 0.0, NEG)


def each(refs):
    return [ref.at[k] for ref in refs for k in range(ref.shape[0])]


def stack_heads(ref, kv):
    return jnp.concatenate(
        [ref[:, (kv * 4 + g) * HEAD:(kv * 4 + g + 1) * HEAD] for g in range(4)], axis=0
    )


STEP = 256


def attend(kv, q, top, total, acc, kv_scr, bias_scr, s_scr):
    count = kv_scr.shape[0] // STEP

    def scores(i, best):
        rows = pl.ds(pl.multiple_of(i * STEP, STEP), STEP)
        bias = bias_scr[rows, :]
        s = nt(kv_scr[rows, kv * HEAD:(kv + 1) * HEAD], q)
        s = s + jnp.concatenate([bias] * 4, axis=1)
        s_scr[rows, :] = s
        return jnp.maximum(best, jnp.max(s.reshape(STEP // 8, 8, 512), axis=0))

    best = lax.fori_loop(0, count, scores, jnp.broadcast_to(top, (8, 512)), unroll=True)
    best = jnp.max(best, axis=0, keepdims=True)
    factor = jnp.exp2((top - best) * (SCALE * LOG2E))

    def values(i, state):
        sums, acc = state
        rows = pl.ds(pl.multiple_of(i * STEP, STEP), STEP)
        p = jnp.exp2((s_scr[rows, :] - best) * (SCALE * LOG2E))
        v = kv_scr[rows, 256 + kv * HEAD:256 + (kv + 1) * HEAD]
        sums = sums + jnp.sum(p.reshape(STEP // 8, 8, 512), axis=0)
        return sums, acc + tn(v, p.astype(BF16))

    sums, acc = lax.fori_loop(0, count, values, (jnp.zeros((8, 512), F32), acc * factor), unroll=True)
    return best, total * factor + jnp.sum(sums, axis=0, keepdims=True), acc


def forward_kernel(own_ref, q_ref, *refs):
    pieces, (o_ref, lse_ref, kv_scr, bias_scr, s_scr) = each(refs[:2]), refs[2:]
    fill(own_ref, pieces, kv_scr, bias_scr)
    for kv in range(2):
        top, total, acc = attend(
            kv, stack_heads(q_ref, kv), jnp.full((1, 512), NEG, F32), jnp.zeros((1, 512), F32),
            jnp.zeros((HEAD, 512), F32), kv_scr, bias_scr, s_scr,
        )
        out = (acc / total).T.astype(BF16)
        for g in range(4):
            o_ref[:, (kv * 4 + g) * HEAD:(kv * 4 + g + 1) * HEAD] = out[g * ROWS:(g + 1) * ROWS]
        lse = top * (SCALE * LOG2E) + jnp.log2(total)
        lse_ref[kv] = jnp.broadcast_to(lse, (8, 512))


def backward_kernel(own_ref, q_ref, d_ref, o_ref, lse_ref, *refs):
    dq_ref, own_out, sib_out, kv_scr, bias_scr = refs[2:]
    fill(own_ref, each(refs[:2]), kv_scr, bias_scr)
    for kv in range(2):
        q = stack_heads(q_ref, kv)
        d = stack_heads(d_ref, kv)
        o = stack_heads(o_ref, kv)
        lse = lse_ref[kv, :1, :]
        product = d.astype(F32) * o.astype(F32)
        delta = jnp.sum(product.T, axis=0, keepdims=True)

        def half(out_ref, part, base):
            def tile(i, acc):
                rows = pl.ds(pl.multiple_of(base + i * STEP, STEP), STEP)
                k = kv_scr[rows, kv * HEAD:(kv + 1) * HEAD]
                v = kv_scr[rows, 256 + kv * HEAD:256 + (kv + 1) * HEAD]
                bias = bias_scr[rows, :]
                s = nt(k, q) * (SCALE * LOG2E) - lse
                p = jnp.exp2(s + jnp.concatenate([bias] * 4, axis=1))
                dp = nt(v, d)
                ds = (p * (dp - delta)).astype(BF16)
                dk = (nn(ds, q) * SCALE).astype(BF16)
                dv = nn(p.astype(BF16), d).astype(BF16)
                for h in range(2):
                    at = slice(h * ROWS, (h + 1) * ROWS)
                    out_ref[2 * i + h, part, :, kv * HEAD:(kv + 1) * HEAD] = dk[at]
                    out_ref[2 * i + h, part, :, 256 + kv * HEAD:256 + (kv + 1) * HEAD] = dv[at]
                return acc + tn(k, ds)

            return tile

        acc = jnp.zeros((HEAD, 512), F32)
        for part in range(2):
            acc = lax.fori_loop(0, 2, half(own_out, part, part * 512), acc, unroll=True)
            acc = lax.fori_loop(0, 2, half(sib_out, part, part * 512 + 1024), acc, unroll=True)
        dq = (acc * SCALE).T
        for g in range(4):
            dq_ref[:, (kv * 4 + g) * HEAD:(kv * 4 + g + 1) * HEAD] = dq[g * ROWS:(g + 1) * ROWS]


def weight_kernel(rel, z_ref, *refs):
    heads, grads, (out_ref, h_scr, g_scr) = refs[:4], refs[4:8], refs[8:]
    z = z_ref[0]
    for n in range(4):
        rows = slice(n * ROWS, (n + 1) * ROWS)
        h_scr[rows, :] = heads[n][...]
        for part in range(2):
            g_scr[part, rows, :] = grads[n][rel, part]

    def piece(k, carry):
        to = (z + k) % 8
        lanes = pl.ds(pl.multiple_of((to % 4) * 256, 256), 256)
        out_ref[k] = tn(h_scr[:, lanes], g_scr[to // 4]).astype(BF16)
        return carry

    lax.fori_loop(0, 8, piece, 0, unroll=True)


def select_kernel(at_ref, g0, g1, g2, g3, o0, o1, o2, o3, scr):
    x, c, y = at_ref[0], at_ref[1], at_ref[2]
    for k, g in enumerate((g0, g1, g2, g3)):
        scr[y ^ k] = g[...]
    for k, out in enumerate((o0, o1, o2, o3)):
        to = x ^ k
        for rel in range(2):
            lane = ((to % 2) * 2 + (c + rel) % 2) * 256
            for part in range(2):
                out[rel, part] = scr[part * 2 + to // 2, :, pl.ds(pl.multiple_of(lane, 256), 256)]


def weight_copies(places, w_ref, w_scr, sems):
    copies = []
    for k, place in enumerate(places):
        columns = pl.ds(pl.multiple_of(place * 1024, 1024), 1024)
        copies.append(pltpu.make_async_copy(w_ref.at[:, columns], w_scr.at[k], sems.at[k]))
    for copy in copies:
        copy.start()
    return copies


def grad_heads_kernel(at_ref, g0, g1, g2, g3, w_ref, out_ref, w_scr, sems):
    copies = weight_copies([at_ref[2] ^ k for k in range(4)], w_ref, w_scr, sems)
    acc = jnp.zeros(out_ref.shape, F32)
    for k, g in enumerate((g0, g1, g2, g3)):
        copies[k].wait()
        acc = acc + nt(g[...], w_scr[k])
    out_ref[...] = acc.astype(BF16)


def project_kernel(at_ref, h_ref, w_ref, own_ref, far_ref, w_scr, sems):
    y = at_ref[2]
    copies = weight_copies([y ^ bits for bits in (3, 2, 0, 1)], w_ref, w_scr, sems)
    h = h_ref[...]
    for k in range(4):
        copies[k].wait()
        out = far_ref if k < 2 else own_ref
        out[k % 2] = nn(h, w_scr[k]).astype(out.dtype)


def spread_kernel(at_ref, p0, p1, p2, p3, out_ref):
    for k, p in enumerate((p0, p1, p2, p3)):
        rows = pl.ds(pl.multiple_of((at_ref[3] ^ k) * 256, 256), 256)
        out_ref[rows, :] = p[...].astype(F32)


SMEM = pl.BlockSpec(memory_space=pltpu.SMEM)
VMEM = pl.BlockSpec(memory_space=pltpu.VMEM)


ANY = pl.BlockSpec(memory_space=pl.ANY)


def call(kernel, inputs, out_shape, scratch, time, anywhere=(), first=SMEM, limit=VMEM_LIMIT):
    specs = [first] + [ANY if n in anywhere else VMEM for n in range(1, len(inputs))]
    return pl.pallas_call(
        kernel,
        out_shape=out_shape,
        in_specs=specs,
        out_specs=jax.tree.map(lambda _: VMEM, out_shape),
        scratch_shapes=scratch,
        compiler_params=pltpu.CompilerParams(vmem_limit_bytes=limit),
        cost_estimate=pl.CostEstimate(
            flops=int(time * 6e9), bytes_accessed=1 << 20, transcendentals=0
        ),
    )(*inputs)


def y_swap(value, bits):
    return lax.ppermute(value, "head", [(i, i ^ bits) for i in range(4)])


def z_shift(value, by):
    pairs = []
    for at in range(8):
        to = (at + by) % 8
        for r in range(8):
            pairs.append(((at % 4) * 16 + (at // 4) * 8 + r, (to % 4) * 16 + (to // 4) * 8 + r))
    return lax.ppermute(value, ("dp", "seq"), pairs)


def together(*values):
    return lax.optimization_barrier(values)


def after(value, *others):
    return lax.optimization_barrier((value, *others))[0]


def added(*parts):
    total = parts[0].astype(F32)
    for part in parts[1:]:
        total = total + part.astype(F32)
    return total


def shards(queries, keys, values, grad_out, doc_ids, out_weight):
    rows = queries.shape[1]
    depth = out_weight.shape[0]
    index = lax.axis_index("seq")
    layer = lax.axis_index("dp")
    y = lax.axis_index("head")
    z, x, c = index // 8, (index // 2) % 4, index % 2
    own = index.astype(jnp.int32).reshape(1)
    height = (z * 4 + layer).astype(jnp.int32).reshape(1)
    place = jnp.stack([x, c, y, layer]).astype(jnp.int32)
    shape = jax.ShapeDtypeStruct

    message = call(
        message_kernel, [doc_ids, keys[0], values[0]], shape((rows + 16, 512), BF16),
        [pltpu.VMEM((1, rows), jnp.int32), pltpu.SemaphoreType.DMA((3,))], 0.5, (1, 2), ANY,
        60 * 1024 * 1024,
    )
    q = queries[0]
    w_scratch = [pltpu.VMEM((4, 1024, 1024), BF16), pltpu.SemaphoreType.DMA((4,))]
    cotangent = after(grad_out[0], message)
    *crossed, across, near1, near3 = together(
        *[y_swap(cotangent, k) for k in (1, 3)], z_swap(message),
        *[x_swap(message, k) for k in (1, 3)],
    )
    cotangents = [grad_out[0], crossed[0], y_swap(after(grad_out[0], across), 2), crossed[1]]

    chosen = call(
        select_kernel, [place] + cotangents, (shape((2, 2, rows, 256), BF16),) * 4,
        [pltpu.VMEM((4, rows, 1024), BF16)], 1.5,
    )
    near2, far1, far3, far2, *chosen = together(
        x_swap(message, 2), *[x_swap(across, k) for k in (1, 3, 2)],
        *chosen,
    )

    pieces = jnp.stack([message, near1, near2, near3, across, far1, far2, far3])
    theirs, *chosen = together(core_swap(pieces), *chosen)
    pieces = [pieces, theirs]
    heads, lse = call(
        forward_kernel, [own, q] + pieces,
        (shape((rows, depth), BF16), shape((2, 8, 512), F32)),
        [
            pltpu.VMEM((2048, 512), BF16),
            pltpu.VMEM((2048, ROWS), F32),
            pltpu.VMEM((2048, 512), F32),
        ],
        4,
    )
    head_grad = call(
        grad_heads_kernel, [after(place, theirs)] + cotangents + [out_weight], shape((rows, depth), BF16),
        w_scratch, 6, (5,),
    )
    heads, head_grad, *grads = together(
        heads, head_grad, *[x_swap(chosen[k], k) for k in (3, 2, 1)]
    )
    grads = [chosen[0]] + grads[::-1]

    grad_query, kept, given = call(
        backward_kernel, [own, q, head_grad, heads, lse] + pieces,
        (shape((rows, depth), F32), shape((4, 2, rows, 512), BF16), shape((4, 2, rows, 512), BF16)),
        [pltpu.VMEM((2048, 512), BF16), pltpu.VMEM((2048, ROWS), F32)], 11,
    )
    terms = call(
        project_kernel, [place, heads, out_weight],
        (shape((2, rows, 1024), F32), shape((2, rows, 1024), BF16)), w_scratch, 5, (2,),
    )
    kept, given, own_terms, far_terms, *close = together(
        kept, given, *terms, *[x_swap(heads, k) for k in (3, 2, 1)]
    )
    close = close[::-1]
    far_terms = y_swap(far_terms, 3)
    close = [heads] + close

    def products(rel):
        return call(
            functools.partial(weight_kernel, rel), [height] + close + grads,
            shape((8, 256, 256), BF16),
            [pltpu.VMEM((512, depth), BF16), pltpu.VMEM((2, 512, 256), BF16)], 1,
        )

    summed = added(kept, core_swap(given)).astype(BF16)
    theirs = core_swap(products(1))
    ours, theirs, summed = together(products(0), theirs, summed)

    up, down = added(ours[4], theirs[4]).astype(BF16), added(ours[5], theirs[5]).astype(BF16)
    back, *rest = [x_swap(summed[k], k) for k in (1, 3, 2)]
    for k in range(3):
        up = added(z_shift(up, 1), ours[3 - k], theirs[3 - k]).astype(BF16)
        down = z_shift(down, -1)
        if k < 2:
            down = added(down, ours[6 + k], theirs[6 + k]).astype(BF16)
        if k == 1:
            up, down, back = together(up, down, back)
        if k == 0:
            up, down, far_terms = together(up, down, far_terms)
            halves = own_terms + far_terms.astype(F32)
            far_terms = y_swap(halves[1].astype(BF16), 1)
        if k == 2:
            up, down, *rest = together(up, down, *rest)
    along = added(summed[0], back, *rest)
    block = added(z_shift(up, 1), down, ours[0], theirs[0]).astype(BF16)
    block, far_terms, far_keys = together(
        block, far_terms, z_swap(along[1].astype(BF16))
    )
    layer_out = halves[0] + far_terms.astype(F32)

    blocks = [lax.ppermute(block, "dp", [(i, i ^ k) for i in range(4)]) for k in (2, 1, 3)]
    blocks = [block, blocks[1], blocks[0], blocks[2]]
    final = along[0] + far_keys.astype(F32)
    weight_grad = call(spread_kernel, [place] + blocks, shape((1024, 256), F32), [], 1)
    return (
        layer_out[None],
        grad_query[None],
        final[:, :256][None],
        final[:, 256:][None],
        weight_grad,
    )


def solution(mesh):
    placed = (
        P("dp", "seq", "head"),
        P("dp", "seq", "head"),
        P("dp", "seq", "head"),
        P("dp", "seq", "head"),
        P("dp", "seq"),
        P("head", None),
    )
    return jax.shard_map(
        shards,
        mesh=mesh,
        in_specs=placed,
        out_specs=(
            P("dp", "seq", "head"),
            P("dp", "seq", "head"),
            P("dp", "seq", "head"),
            P("dp", "seq", "head"),
            P("head", "seq"),
        ),
        check_vma=False,
    )
```

```python
import functools

import jax
import jax.numpy as jnp
from jax import lax
from jax.experimental import pallas as pl
from jax.experimental.pallas import tpu as pltpu
from jax.sharding import PartitionSpec as P

HEAD = 128
ROWS = 128
NEG = -1e30
SCALE = HEAD ** -0.5
LOG2E = 1.4426950408889634
F32 = jnp.float32
BF16 = jnp.bfloat16
VMEM_LIMIT = 48 * 1024 * 1024


def seq_perm(move):
    pairs = []
    for s in range(16):
        z, x, c = s // 8, (s // 2) % 4, s % 2
        nz, nx, nc = move(z, x, c)
        pairs.append((s, nz * 8 + nx * 2 + nc))
    return pairs


def core_swap(value):
    return lax.ppermute(value, "seq", seq_perm(lambda z, x, c: (z, x, 1 - c)))


def x_swap(value, bits):
    return lax.ppermute(value, "seq", seq_perm(lambda z, x, c: (z, x ^ bits, c)))


def z_swap(value):
    return lax.ppermute(value, "seq", seq_perm(lambda z, x, c: (1 - z, x, c)))


def nt(a, b):
    return lax.dot_general(a, b, (((1,), (1,)), ((), ())), preferred_element_type=F32)


def nn(a, b):
    return lax.dot_general(a, b, (((1,), (0,)), ((), ())), preferred_element_type=F32)


def tn(a, b):
    return lax.dot_general(a, b, (((0,), (0,)), ((), ())), preferred_element_type=F32)


def message_kernel(doc_ref, k_ref, v_ref, out_ref, doc_scr, sems):
    copies = [
        pltpu.make_async_copy(doc_ref, doc_scr, sems.at[0]),
        pltpu.make_async_copy(k_ref, out_ref.at[:ROWS, :256], sems.at[1]),
        pltpu.make_async_copy(v_ref, out_ref.at[:ROWS, 256:], sems.at[2]),
    ]
    for copy in copies:
        copy.start()
    copies[0].wait()
    docs = jnp.broadcast_to(doc_scr[...].astype(F32), (16, ROWS)).astype(BF16)
    for n in range(4):
        out_ref[ROWS:, n * ROWS:(n + 1) * ROWS] = docs
    copies[1].wait()
    copies[2].wait()


def fill(own_ref, pieces, kv_scr, bias_scr):
    own = own_ref[0]
    z, x, c = own // 8, (own // 2) % 4, own % 2
    key_at = lax.broadcasted_iota(jnp.int32, (ROWS, ROWS), 0)
    query_at = lax.broadcasted_iota(jnp.int32, (ROWS, ROWS), 1)
    lag = key_at - query_at
    query_doc = pieces[0][ROWS:ROWS + 1, :ROWS].astype(F32)
    for n, piece in enumerate(pieces):
        other, part, k = n // 8, (n // 4) % 2, n % 4
        at = n * ROWS
        kv_scr[at:at + ROWS, :] = piece[:ROWS, :]
        block = ((z + part) % 2) * 8 + (x ^ k) * 2 + (c + other) % 2
        doc = piece[ROWS:ROWS + 8, :ROWS].astype(F32)
        doc = jnp.broadcast_to(doc[:1, :], (ROWS, ROWS)).T
        allowed = (doc == query_doc) & (lag <= (own - block) * ROWS)
        bias_scr[at:at + ROWS, :] = jnp.where(allowed, 0.0, NEG)


def each(refs):
    return [ref.at[k] for ref in refs for k in range(ref.shape[0])]


def stack_heads(ref, kv):
    return jnp.concatenate(
        [ref[:, (kv * 4 + g) * HEAD:(kv * 4 + g + 1) * HEAD] for g in range(4)], axis=0
    )


STEP = 512


def attend(kv, q, top, total, acc, kv_scr, bias_scr, s_scr):
    count = kv_scr.shape[0] // STEP

    def scores(i, best):
        rows = pl.ds(pl.multiple_of(i * STEP, STEP), STEP)
        bias = bias_scr[rows, :]
        s = nt(kv_scr[rows, kv * HEAD:(kv + 1) * HEAD], q)
        s = s + jnp.concatenate([bias] * 4, axis=1)
        s_scr[rows, :] = s
        return jnp.maximum(best, jnp.max(s.reshape(STEP // 8, 8, 512), axis=0))

    best = lax.fori_loop(0, count, scores, jnp.broadcast_to(top, (8, 512)), unroll=True)
    best = jnp.max(best, axis=0, keepdims=True)
    factor = jnp.exp2((top - best) * (SCALE * LOG2E))

    def values(i, state):
        sums, acc = state
        rows = pl.ds(pl.multiple_of(i * STEP, STEP), STEP)
        p = jnp.exp2((s_scr[rows, :] - best) * (SCALE * LOG2E))
        v = kv_scr[rows, 256 + kv * HEAD:256 + (kv + 1) * HEAD]
        sums = sums + jnp.sum(p.reshape(STEP // 8, 8, 512), axis=0)
        return sums, acc + tn(v, p.astype(BF16))

    sums, acc = lax.fori_loop(0, count, values, (jnp.zeros((8, 512), F32), acc * factor), unroll=True)
    return best, total * factor + jnp.sum(sums, axis=0, keepdims=True), acc


def forward_kernel(own_ref, q_ref, *refs):
    pieces, (o_ref, lse_ref, kv_scr, bias_scr, s_scr) = each(refs[:2]), refs[2:]
    fill(own_ref, pieces, kv_scr, bias_scr)
    for kv in range(2):
        top, total, acc = attend(
            kv, stack_heads(q_ref, kv), jnp.full((1, 512), NEG, F32), jnp.zeros((1, 512), F32),
            jnp.zeros((HEAD, 512), F32), kv_scr, bias_scr, s_scr,
        )
        out = (acc / total).T.astype(BF16)
        for g in range(4):
            o_ref[:, (kv * 4 + g) * HEAD:(kv * 4 + g + 1) * HEAD] = out[g * ROWS:(g + 1) * ROWS]
        lse = top * (SCALE * LOG2E) + jnp.log2(total)
        lse_ref[kv] = jnp.broadcast_to(lse, (8, 512))


def backward_kernel(own_ref, q_ref, d_ref, o_ref, lse_ref, *refs):
    dq_ref, own_out, sib_out, kv_scr, bias_scr = refs[2:]
    fill(own_ref, each(refs[:2]), kv_scr, bias_scr)
    for kv in range(2):
        q = stack_heads(q_ref, kv)
        d = stack_heads(d_ref, kv)
        o = stack_heads(o_ref, kv)
        lse = lse_ref[kv, :1, :]
        product = d.astype(F32) * o.astype(F32)
        delta = jnp.sum(product.T, axis=0, keepdims=True)

        def half(out_ref, part, base):
            def tile(i, acc):
                rows = pl.ds(pl.multiple_of(base + i * STEP, STEP), STEP)
                k = kv_scr[rows, kv * HEAD:(kv + 1) * HEAD]
                v = kv_scr[rows, 256 + kv * HEAD:256 + (kv + 1) * HEAD]
                bias = bias_scr[rows, :]
                s = nt(k, q) * (SCALE * LOG2E) - lse
                p = jnp.exp2(s + jnp.concatenate([bias] * 4, axis=1))
                dp = nt(v, d)
                ds = (p * (dp - delta)).astype(BF16)
                dk = (nn(ds, q) * SCALE).astype(BF16)
                dv = nn(p.astype(BF16), d).astype(BF16)
                for h in range(4):
                    at = slice(h * ROWS, (h + 1) * ROWS)
                    out_ref[4 * i + h, part, :, kv * HEAD:(kv + 1) * HEAD] = dk[at]
                    out_ref[4 * i + h, part, :, 256 + kv * HEAD:256 + (kv + 1) * HEAD] = dv[at]
                return acc + tn(k, ds)

            return tile

        acc = jnp.zeros((HEAD, 512), F32)
        for part in range(2):
            acc = lax.fori_loop(0, 1, half(own_out, part, part * 512), acc, unroll=True)
            acc = lax.fori_loop(0, 1, half(sib_out, part, part * 512 + 1024), acc, unroll=True)
        dq = (acc * SCALE).T
        for g in range(4):
            dq_ref[:, (kv * 4 + g) * HEAD:(kv * 4 + g + 1) * HEAD] = dq[g * ROWS:(g + 1) * ROWS]


def weight_kernel(rel, z_ref, *refs):
    heads, grads, (out_ref, h_scr, g_scr) = refs[:4], refs[4:8], refs[8:]
    z = z_ref[0]
    for n in range(4):
        rows = slice(n * ROWS, (n + 1) * ROWS)
        h_scr[rows, :] = heads[n][...]
        for part in range(2):
            g_scr[part, rows, :] = grads[n][rel, part]

    def piece(k, carry):
        to = (z + k) % 8
        lanes = pl.ds(pl.multiple_of((to % 4) * 256, 256), 256)
        out_ref[k] = tn(h_scr[:, lanes], g_scr[to // 4]).astype(BF16)
        return carry

    lax.fori_loop(0, 8, piece, 0, unroll=True)


def select_kernel(at_ref, g0, g1, g2, g3, o0, o1, o2, o3, scr):
    x, c, y = at_ref[0], at_ref[1], at_ref[2]
    for k, g in enumerate((g0, g1, g2, g3)):
        scr[y ^ k] = g[...]
    for k, out in enumerate((o0, o1, o2, o3)):
        to = x ^ k
        for rel in range(2):
            lane = ((to % 2) * 2 + (c + rel) % 2) * 256
            for part in range(2):
                out[rel, part] = scr[part * 2 + to // 2, :, pl.ds(pl.multiple_of(lane, 256), 256)]


def weight_copies(places, w_ref, w_scr, sems):
    copies = []
    for k, place in enumerate(places):
        columns = pl.ds(pl.multiple_of(place * 1024, 1024), 1024)
        copies.append(pltpu.make_async_copy(w_ref.at[:, columns], w_scr.at[k], sems.at[k]))
    for copy in copies:
        copy.start()
    return copies


def grad_heads_kernel(at_ref, g0, g1, g2, g3, w_ref, out_ref, w_scr, sems):
    copies = weight_copies([at_ref[2] ^ k for k in range(4)], w_ref, w_scr, sems)
    acc = jnp.zeros(out_ref.shape, F32)
    for k, g in enumerate((g0, g1, g2, g3)):
        copies[k].wait()
        acc = acc + nt(g[...], w_scr[k])
    out_ref[...] = acc.astype(BF16)


def project_kernel(at_ref, h_ref, w_ref, own_ref, far_ref, w_scr, sems):
    y = at_ref[2]
    copies = weight_copies([y ^ bits for bits in (3, 2, 0, 1)], w_ref, w_scr, sems)
    h = h_ref[...]
    for k in range(4):
        copies[k].wait()
        out = far_ref if k < 2 else own_ref
        out[k % 2] = nn(h, w_scr[k]).astype(out.dtype)


def spread_kernel(at_ref, p0, p1, p2, p3, out_ref):
    for k, p in enumerate((p0, p1, p2, p3)):
        rows = pl.ds(pl.multiple_of((at_ref[3] ^ k) * 256, 256), 256)
        out_ref[rows, :] = p[...].astype(F32)


SMEM = pl.BlockSpec(memory_space=pltpu.SMEM)
VMEM = pl.BlockSpec(memory_space=pltpu.VMEM)


ANY = pl.BlockSpec(memory_space=pl.ANY)


def call(kernel, inputs, out_shape, scratch, time, anywhere=(), first=SMEM, limit=VMEM_LIMIT):
    specs = [first] + [ANY if n in anywhere else VMEM for n in range(1, len(inputs))]
    return pl.pallas_call(
        kernel,
        out_shape=out_shape,
        in_specs=specs,
        out_specs=jax.tree.map(lambda _: VMEM, out_shape),
        scratch_shapes=scratch,
        compiler_params=pltpu.CompilerParams(vmem_limit_bytes=limit),
        cost_estimate=pl.CostEstimate(
            flops=int(time * 6e9), bytes_accessed=1 << 20, transcendentals=0
        ),
    )(*inputs)


def y_swap(value, bits):
    return lax.ppermute(value, "head", [(i, i ^ bits) for i in range(4)])


def z_shift(value, by):
    pairs = []
    for at in range(8):
        to = (at + by) % 8
        for r in range(8):
            pairs.append(((at % 4) * 16 + (at // 4) * 8 + r, (to % 4) * 16 + (to // 4) * 8 + r))
    return lax.ppermute(value, ("dp", "seq"), pairs)


def together(*values):
    return lax.optimization_barrier(values)


def after(value, *others):
    return lax.optimization_barrier((value, *others))[0]


def added(*parts):
    total = parts[0].astype(F32)
    for part in parts[1:]:
        total = total + part.astype(F32)
    return total


def shards(queries, keys, values, grad_out, doc_ids, out_weight):
    rows = queries.shape[1]
    depth = out_weight.shape[0]
    index = lax.axis_index("seq")
    layer = lax.axis_index("dp")
    y = lax.axis_index("head")
    z, x, c = index // 8, (index // 2) % 4, index % 2
    own = index.astype(jnp.int32).reshape(1)
    height = (z * 4 + layer).astype(jnp.int32).reshape(1)
    place = jnp.stack([x, c, y, layer]).astype(jnp.int32)
    shape = jax.ShapeDtypeStruct

    message = call(
        message_kernel, [doc_ids, keys[0], values[0]], shape((rows + 16, 512), BF16),
        [pltpu.VMEM((1, rows), jnp.int32), pltpu.SemaphoreType.DMA((3,))], 0.5, (1, 2), ANY,
        60 * 1024 * 1024,
    )
    q = queries[0]
    w_scratch = [pltpu.VMEM((4, 1024, 1024), BF16), pltpu.SemaphoreType.DMA((4,))]
    cotangent = after(grad_out[0], message)
    *crossed, across, near1, near3 = together(
        *[y_swap(cotangent, k) for k in (1, 3)], z_swap(message),
        *[x_swap(message, k) for k in (1, 3)],
    )
    cotangents = [grad_out[0], crossed[0], y_swap(after(grad_out[0], across), 2), crossed[1]]

    chosen = call(
        select_kernel, [place] + cotangents, (shape((2, 2, rows, 256), BF16),) * 4,
        [pltpu.VMEM((4, rows, 1024), BF16)], 1.5,
    )
    near2, far1, far3, far2, *chosen = together(
        x_swap(message, 2), *[x_swap(across, k) for k in (1, 3, 2)],
        *chosen,
    )

    pieces = jnp.stack([message, near1, near2, near3, across, far1, far2, far3])
    theirs, *chosen = together(core_swap(pieces), *chosen)
    pieces = [pieces, theirs]
    heads, lse = call(
        forward_kernel, [own, q] + pieces,
        (shape((rows, depth), BF16), shape((2, 8, 512), F32)),
        [
            pltpu.VMEM((2048, 512), BF16),
            pltpu.VMEM((2048, ROWS), F32),
            pltpu.VMEM((2048, 512), F32),
        ],
        4,
    )
    head_grad = call(
        grad_heads_kernel, [after(place, theirs)] + cotangents + [out_weight], shape((rows, depth), BF16),
        w_scratch, 6, (5,),
    )
    heads, head_grad, *grads = together(
        heads, head_grad, *[x_swap(chosen[k], k) for k in (3, 2, 1)]
    )
    grads = [chosen[0]] + grads[::-1]

    grad_query, kept, given = call(
        backward_kernel, [own, q, head_grad, heads, lse] + pieces,
        (shape((rows, depth), F32), shape((4, 2, rows, 512), BF16), shape((4, 2, rows, 512), BF16)),
        [pltpu.VMEM((2048, 512), BF16), pltpu.VMEM((2048, ROWS), F32)], 11,
    )
    terms = call(
        project_kernel, [place, heads, out_weight],
        (shape((2, rows, 1024), F32), shape((2, rows, 1024), BF16)), w_scratch, 5, (2,),
    )
    kept, given, own_terms, far_terms, *close = together(
        kept, given, *terms, *[x_swap(heads, k) for k in (3, 2, 1)]
    )
    close = close[::-1]
    far_terms = y_swap(far_terms, 3)
    close = [heads] + close

    def products(rel):
        return call(
            functools.partial(weight_kernel, rel), [height] + close + grads,
            shape((8, 256, 256), BF16),
            [pltpu.VMEM((512, depth), BF16), pltpu.VMEM((2, 512, 256), BF16)], 1,
        )

    summed = added(kept, core_swap(given)).astype(BF16)
    theirs = core_swap(products(1))
    ours, theirs, summed = together(products(0), theirs, summed)

    up, down = added(ours[4], theirs[4]).astype(BF16), added(ours[5], theirs[5]).astype(BF16)
    back, *rest = [x_swap(summed[k], k) for k in (1, 3, 2)]
    for k in range(3):
        up = added(z_shift(up, 1), ours[3 - k], theirs[3 - k]).astype(BF16)
        down = z_shift(down, -1)
        if k < 2:
            down = added(down, ours[6 + k], theirs[6 + k]).astype(BF16)
        if k == 1:
            up, down, back, *rest = together(up, down, back, *rest)
            along = added(summed[0], back, *rest)
            far_keys = z_swap(along[1].astype(BF16))
        if k == 0:
            up, down, far_terms = together(up, down, far_terms)
            halves = own_terms + far_terms.astype(F32)
            far_terms = y_swap(halves[1].astype(BF16), 1)
        if k == 2:
            up, down = together(up, down)
    block = added(z_shift(up, 1), down, ours[0], theirs[0]).astype(BF16)
    block, far_terms, far_keys = together(block, far_terms, far_keys)
    layer_out = halves[0] + far_terms.astype(F32)

    blocks = [lax.ppermute(block, "dp", [(i, i ^ k) for i in range(4)]) for k in (2, 1, 3)]
    blocks = [block, blocks[1], blocks[0], blocks[2]]
    final = along[0] + far_keys.astype(F32)
    weight_grad = call(spread_kernel, [place] + blocks, shape((1024, 256), F32), [], 1)
    return (
        layer_out[None],
        grad_query[None],
        final[:, :256][None],
        final[:, 256:][None],
        weight_grad,
    )


def solution(mesh):
    placed = (
        P("dp", "seq", "head"),
        P("dp", "seq", "head"),
        P("dp", "seq", "head"),
        P("dp", "seq", "head"),
        P("dp", "seq"),
        P("head", None),
    )
    return jax.shard_map(
        shards,
        mesh=mesh,
        in_specs=placed,
        out_specs=(
            P("dp", "seq", "head"),
            P("dp", "seq", "head"),
            P("dp", "seq", "head"),
            P("dp", "seq", "head"),
            P("head", "seq"),
        ),
        check_vma=False,
    )
```

```python
import functools

import jax
import jax.numpy as jnp
from jax import lax
from jax.experimental import pallas as pl
from jax.experimental.pallas import tpu as pltpu
from jax.sharding import PartitionSpec as P

HEAD = 128
ROWS = 128
NEG = -1e30
SCALE = HEAD ** -0.5
LOG2E = 1.4426950408889634
F32 = jnp.float32
BF16 = jnp.bfloat16
VMEM_LIMIT = 48 * 1024 * 1024


def seq_perm(move):
    pairs = []
    for s in range(16):
        z, x, c = s // 8, (s // 2) % 4, s % 2
        nz, nx, nc = move(z, x, c)
        pairs.append((s, nz * 8 + nx * 2 + nc))
    return pairs


def core_swap(value):
    return lax.ppermute(value, "seq", seq_perm(lambda z, x, c: (z, x, 1 - c)))


def x_swap(value, bits):
    return lax.ppermute(value, "seq", seq_perm(lambda z, x, c: (z, x ^ bits, c)))


def z_swap(value):
    return lax.ppermute(value, "seq", seq_perm(lambda z, x, c: (1 - z, x, c)))


def nt(a, b):
    return lax.dot_general(a, b, (((1,), (1,)), ((), ())), preferred_element_type=F32)


def nn(a, b):
    return lax.dot_general(a, b, (((1,), (0,)), ((), ())), preferred_element_type=F32)


def tn(a, b):
    return lax.dot_general(a, b, (((0,), (0,)), ((), ())), preferred_element_type=F32)


def message_kernel(doc_ref, k_ref, v_ref, out_ref, doc_scr, sems):
    copies = [
        pltpu.make_async_copy(doc_ref, doc_scr, sems.at[0]),
        pltpu.make_async_copy(k_ref, out_ref.at[:ROWS, :256], sems.at[1]),
        pltpu.make_async_copy(v_ref, out_ref.at[:ROWS, 256:], sems.at[2]),
    ]
    for copy in copies:
        copy.start()
    copies[0].wait()
    docs = jnp.broadcast_to(doc_scr[...].astype(F32), (16, ROWS)).astype(BF16)
    for n in range(4):
        out_ref[ROWS:, n * ROWS:(n + 1) * ROWS] = docs
    copies[1].wait()
    copies[2].wait()


def fill(own_ref, pieces, kv_scr, bias_scr):
    own = own_ref[0]
    z, x, c = own // 8, (own // 2) % 4, own % 2
    key_at = lax.broadcasted_iota(jnp.int32, (ROWS, ROWS), 0)
    query_at = lax.broadcasted_iota(jnp.int32, (ROWS, ROWS), 1)
    lag = key_at - query_at
    query_doc = pieces[0][ROWS:ROWS + 1, :ROWS].astype(F32)
    for n, piece in enumerate(pieces):
        other, part, k = n // 8, (n // 4) % 2, n % 4
        at = n * ROWS
        kv_scr[at:at + ROWS, :] = piece[:ROWS, :]
        block = ((z + part) % 2) * 8 + (x ^ k) * 2 + (c + other) % 2
        doc = piece[ROWS:ROWS + 8, :ROWS].astype(F32)
        doc = jnp.broadcast_to(doc[:1, :], (ROWS, ROWS)).T
        allowed = (doc == query_doc) & (lag <= (own - block) * ROWS)
        bias_scr[at:at + ROWS, :] = jnp.where(allowed, 0.0, NEG)


def each(refs):
    return [ref.at[k] for ref in refs for k in range(ref.shape[0])]


def stack_heads(ref, kv):
    return jnp.concatenate(
        [ref[:, (kv * 4 + g) * HEAD:(kv * 4 + g + 1) * HEAD] for g in range(4)], axis=0
    )


STEP = 512


def attend(kv, q, top, total, acc, kv_scr, bias_scr, s_scr):
    count = kv_scr.shape[0] // STEP

    def scores(i, best):
        rows = pl.ds(pl.multiple_of(i * STEP, STEP), STEP)
        bias = bias_scr[rows, :]
        s = nt(kv_scr[rows, kv * HEAD:(kv + 1) * HEAD], q)
        s = s + jnp.concatenate([bias] * 4, axis=1)
        s_scr[rows, :] = s
        return jnp.maximum(best, jnp.max(s.reshape(STEP // 8, 8, 512), axis=0))

    best = lax.fori_loop(0, count, scores, jnp.broadcast_to(top, (8, 512)), unroll=True)
    best = jnp.max(best, axis=0, keepdims=True)
    factor = jnp.exp2((top - best) * (SCALE * LOG2E))

    def values(i, state):
        sums, acc = state
        rows = pl.ds(pl.multiple_of(i * STEP, STEP), STEP)
        p = jnp.exp2((s_scr[rows, :] - best) * (SCALE * LOG2E))
        v = kv_scr[rows, 256 + kv * HEAD:256 + (kv + 1) * HEAD]
        sums = sums + jnp.sum(p.reshape(STEP // 8, 8, 512), axis=0)
        return sums, acc + tn(v, p.astype(BF16))

    sums, acc = lax.fori_loop(0, count, values, (jnp.zeros((8, 512), F32), acc * factor), unroll=True)
    return best, total * factor + jnp.sum(sums, axis=0, keepdims=True), acc


def forward_kernel(own_ref, q_ref, *refs):
    pieces, (o_ref, lse_ref, kv_scr, bias_scr, s_scr) = each(refs[:2]), refs[2:]
    fill(own_ref, pieces, kv_scr, bias_scr)
    for kv in range(2):
        top, total, acc = attend(
            kv, stack_heads(q_ref, kv), jnp.full((1, 512), NEG, F32), jnp.zeros((1, 512), F32),
            jnp.zeros((HEAD, 512), F32), kv_scr, bias_scr, s_scr,
        )
        out = (acc / total).T.astype(BF16)
        for g in range(4):
            o_ref[:, (kv * 4 + g) * HEAD:(kv * 4 + g + 1) * HEAD] = out[g * ROWS:(g + 1) * ROWS]
        lse = top * (SCALE * LOG2E) + jnp.log2(total)
        lse_ref[kv] = jnp.broadcast_to(lse, (8, 512))


def backward_kernel(own_ref, q_ref, d_ref, o_ref, lse_ref, *refs):
    dq_ref, own_out, sib_out, kv_scr, bias_scr = refs[2:]
    fill(own_ref, each(refs[:2]), kv_scr, bias_scr)
    for kv in range(2):
        q = stack_heads(q_ref, kv)
        d = stack_heads(d_ref, kv)
        o = stack_heads(o_ref, kv)
        lse = lse_ref[kv, :1, :]
        product = d.astype(F32) * o.astype(F32)
        delta = jnp.sum(product.T, axis=0, keepdims=True)

        def half(out_ref, part, base):
            def tile(i, acc):
                rows = pl.ds(pl.multiple_of(base + i * STEP, STEP), STEP)
                k = kv_scr[rows, kv * HEAD:(kv + 1) * HEAD]
                v = kv_scr[rows, 256 + kv * HEAD:256 + (kv + 1) * HEAD]
                bias = bias_scr[rows, :]
                s = nt(k, q) * (SCALE * LOG2E) - lse
                p = jnp.exp2(s + jnp.concatenate([bias] * 4, axis=1))
                dp = nt(v, d)
                ds = (p * (dp - delta)).astype(BF16)
                dk = (nn(ds, q) * SCALE).astype(BF16)
                dv = nn(p.astype(BF16), d).astype(BF16)
                for h in range(4):
                    at = slice(h * ROWS, (h + 1) * ROWS)
                    out_ref[4 * i + h, part, :, kv * HEAD:(kv + 1) * HEAD] = dk[at]
                    out_ref[4 * i + h, part, :, 256 + kv * HEAD:256 + (kv + 1) * HEAD] = dv[at]
                return acc + tn(k, ds)

            return tile

        acc = jnp.zeros((HEAD, 512), F32)
        for part in range(2):
            acc = lax.fori_loop(0, 1, half(own_out, part, part * 512), acc, unroll=True)
            acc = lax.fori_loop(0, 1, half(sib_out, part, part * 512 + 1024), acc, unroll=True)
        dq = (acc * SCALE).T
        for g in range(4):
            dq_ref[:, (kv * 4 + g) * HEAD:(kv * 4 + g + 1) * HEAD] = dq[g * ROWS:(g + 1) * ROWS]


def weight_kernel(rel, z_ref, *refs):
    heads, grads, (out_ref, h_scr, g_scr) = refs[:4], refs[4:8], refs[8:]
    z = z_ref[0]
    for n in range(4):
        rows = slice(n * ROWS, (n + 1) * ROWS)
        h_scr[rows, :] = heads[n][...]
        for part in range(2):
            g_scr[part, rows, :] = grads[n][rel, part]

    def piece(k, carry):
        to = (z + k) % 8
        lanes = pl.ds(pl.multiple_of((to % 4) * 256, 256), 256)
        out_ref[k] = tn(h_scr[:, lanes], g_scr[to // 4]).astype(BF16)
        return carry

    lax.fori_loop(0, 8, piece, 0, unroll=True)


def select_kernel(at_ref, g0, g1, g2, g3, o0, o1, o2, o3, scr):
    x, c, y = at_ref[0], at_ref[1], at_ref[2]
    for k, g in enumerate((g0, g1, g2, g3)):
        scr[y ^ k] = g[...]
    for k, out in enumerate((o0, o1, o2, o3)):
        to = x ^ k
        for rel in range(2):
            lane = ((to % 2) * 2 + (c + rel) % 2) * 256
            for part in range(2):
                out[rel, part] = scr[part * 2 + to // 2, :, pl.ds(pl.multiple_of(lane, 256), 256)]


def weight_copies(places, w_ref, w_scr, sems):
    copies = []
    for k, place in enumerate(places):
        columns = pl.ds(pl.multiple_of(place * 1024, 1024), 1024)
        copies.append(pltpu.make_async_copy(w_ref.at[:, columns], w_scr.at[k], sems.at[k]))
    for copy in copies:
        copy.start()
    return copies


def grad_heads_kernel(at_ref, g0, g1, g2, g3, w_ref, out_ref, w_scr, sems):
    copies = weight_copies([at_ref[2] ^ k for k in range(4)], w_ref, w_scr, sems)
    acc = jnp.zeros(out_ref.shape, F32)
    for k, g in enumerate((g0, g1, g2, g3)):
        copies[k].wait()
        acc = acc + nt(g[...], w_scr[k])
    out_ref[...] = acc.astype(BF16)


def project_kernel(at_ref, h_ref, w_ref, own_ref, far_ref, w_scr, sems):
    y = at_ref[2]
    copies = weight_copies([y ^ bits for bits in (3, 2, 0, 1)], w_ref, w_scr, sems)
    h = h_ref[...]
    for k in range(4):
        copies[k].wait()
        out = far_ref if k < 2 else own_ref
        out[k % 2] = nn(h, w_scr[k]).astype(out.dtype)


def spread_kernel(at_ref, p0, p1, p2, p3, out_ref):
    for k, p in enumerate((p0, p1, p2, p3)):
        rows = pl.ds(pl.multiple_of((at_ref[3] ^ k) * 256, 256), 256)
        out_ref[rows, :] = p[...].astype(F32)


SMEM = pl.BlockSpec(memory_space=pltpu.SMEM)
VMEM = pl.BlockSpec(memory_space=pltpu.VMEM)


ANY = pl.BlockSpec(memory_space=pl.ANY)


def call(kernel, inputs, out_shape, scratch, time, anywhere=(), first=SMEM, limit=VMEM_LIMIT):
    specs = [first] + [ANY if n in anywhere else VMEM for n in range(1, len(inputs))]
    return pl.pallas_call(
        kernel,
        out_shape=out_shape,
        in_specs=specs,
        out_specs=jax.tree.map(lambda _: VMEM, out_shape),
        scratch_shapes=scratch,
        compiler_params=pltpu.CompilerParams(vmem_limit_bytes=limit),
        cost_estimate=pl.CostEstimate(
            flops=int(time * 6e9), bytes_accessed=1 << 20, transcendentals=0
        ),
    )(*inputs)


def y_swap(value, bits):
    return lax.ppermute(value, "head", [(i, i ^ bits) for i in range(4)])


def z_shift(value, by):
    pairs = []
    for at in range(8):
        to = (at + by) % 8
        for r in range(8):
            pairs.append(((at % 4) * 16 + (at // 4) * 8 + r, (to % 4) * 16 + (to // 4) * 8 + r))
    return lax.ppermute(value, ("dp", "seq"), pairs)


def together(*values):
    return lax.optimization_barrier(values)


def after(value, *others):
    return lax.optimization_barrier((value, *others))[0]


def added(*parts):
    total = parts[0].astype(F32)
    for part in parts[1:]:
        total = total + part.astype(F32)
    return total


def shards(queries, keys, values, grad_out, doc_ids, out_weight):
    rows = queries.shape[1]
    depth = out_weight.shape[0]
    index = lax.axis_index("seq")
    layer = lax.axis_index("dp")
    y = lax.axis_index("head")
    z, x, c = index // 8, (index // 2) % 4, index % 2
    own = index.astype(jnp.int32).reshape(1)
    height = (z * 4 + layer).astype(jnp.int32).reshape(1)
    place = jnp.stack([x, c, y, layer]).astype(jnp.int32)
    shape = jax.ShapeDtypeStruct

    message = call(
        message_kernel, [doc_ids, keys[0], values[0]], shape((rows + 16, 512), BF16),
        [pltpu.VMEM((1, rows), jnp.int32), pltpu.SemaphoreType.DMA((3,))], 0.5, (1, 2), ANY,
        60 * 1024 * 1024,
    )
    q = queries[0]
    w_scratch = [pltpu.VMEM((4, 1024, 1024), BF16), pltpu.SemaphoreType.DMA((4,))]
    cotangent = after(grad_out[0], message)
    *crossed, across, near1, near3 = together(
        *[y_swap(cotangent, k) for k in (1, 3)], z_swap(message),
        *[x_swap(message, k) for k in (1, 3)],
    )
    cotangents = [grad_out[0], crossed[0], y_swap(after(grad_out[0], across), 2), crossed[1]]

    chosen = call(
        select_kernel, [place] + cotangents, (shape((2, 2, rows, 256), BF16),) * 4,
        [pltpu.VMEM((4, rows, 1024), BF16)], 1.5,
    )
    near2, far1, far3, far2, *chosen = together(
        x_swap(message, 2), *[x_swap(across, k) for k in (1, 3, 2)],
        *chosen,
    )

    pieces = jnp.stack([message, near1, near2, near3, across, far1, far2, far3])
    theirs, *chosen = together(core_swap(pieces), *chosen)
    pieces = [pieces, theirs]
    heads, lse = call(
        forward_kernel, [own, q] + pieces,
        (shape((rows, depth), BF16), shape((2, 8, 512), F32)),
        [
            pltpu.VMEM((2048, 512), BF16),
            pltpu.VMEM((2048, ROWS), F32),
            pltpu.VMEM((2048, 512), F32),
        ],
        4,
    )
    head_grad = call(
        grad_heads_kernel, [after(place, theirs)] + cotangents + [out_weight], shape((rows, depth), BF16),
        w_scratch, 6, (5,),
    )
    heads, head_grad, *grads = together(
        heads, head_grad, *[x_swap(chosen[k], k) for k in (3, 2, 1)]
    )
    grads = [chosen[0]] + grads[::-1]

    grad_query, kept, given = call(
        backward_kernel, [own, q, head_grad, heads, lse] + pieces,
        (shape((rows, depth), F32), shape((4, 2, rows, 512), BF16), shape((4, 2, rows, 512), BF16)),
        [pltpu.VMEM((2048, 512), BF16), pltpu.VMEM((2048, ROWS), F32)], 11,
    )
    terms = call(
        project_kernel, [place, heads, out_weight],
        (shape((2, rows, 1024), F32), shape((2, rows, 1024), BF16)), w_scratch, 5, (2,),
    )
    kept, given, own_terms, far_terms, *close = together(
        kept, given, *terms, *[x_swap(heads, k) for k in (3, 2, 1)]
    )
    close = close[::-1]
    far_terms = y_swap(far_terms, 3)
    close = [heads] + close

    def products(rel):
        return call(
            functools.partial(weight_kernel, rel), [height] + close + grads,
            shape((8, 256, 256), BF16),
            [pltpu.VMEM((512, depth), BF16), pltpu.VMEM((2, 512, 256), BF16)], 1,
        )

    summed = added(kept, core_swap(given)).astype(BF16)
    theirs = core_swap(products(1))
    ours, theirs, summed = together(products(0), theirs, summed)

    up, down = added(ours[4], theirs[4]).astype(BF16), added(ours[5], theirs[5]).astype(BF16)
    back, *rest = [x_swap(summed[k], k) for k in (1, 3, 2)]
    for k in range(3):
        up = added(z_shift(up, 1), ours[3 - k], theirs[3 - k]).astype(BF16)
        down = z_shift(down, -1)
        if k < 2:
            down = added(down, ours[6 + k], theirs[6 + k]).astype(BF16)
        if k == 1:
            up, down, back, *rest = together(up, down, back, *rest)
            along = added(summed[0], back, *rest)
            far_keys = z_swap(along[1].astype(BF16))
        if k == 0:
            up, down, far_terms = together(up, down, far_terms)
            halves = own_terms + far_terms.astype(F32)
            far_terms = y_swap(halves[1].astype(BF16), 1)
        if k == 2:
            up, down = together(up, down)
    block = added(z_shift(up, 1), down, ours[0], theirs[0]).astype(BF16)
    block, far_terms, far_keys = together(block, far_terms, far_keys)
    layer_out = halves[0] + far_terms.astype(F32)

    blocks = [lax.ppermute(block, "dp", [(i, i ^ k) for i in range(4)]) for k in (1, 2, 3)]
    blocks = [block, *blocks]
    final = along[0] + far_keys.astype(F32)
    weight_grad = call(spread_kernel, [place] + blocks, shape((1024, 256), F32), [], 1)
    return (
        layer_out[None],
        grad_query[None],
        final[:, :256][None],
        final[:, 256:][None],
        weight_grad,
    )


def solution(mesh):
    placed = (
        P("dp", "seq", "head"),
        P("dp", "seq", "head"),
        P("dp", "seq", "head"),
        P("dp", "seq", "head"),
        P("dp", "seq"),
        P("head", None),
    )
    return jax.shard_map(
        shards,
        mesh=mesh,
        in_specs=placed,
        out_specs=(
            P("dp", "seq", "head"),
            P("dp", "seq", "head"),
            P("dp", "seq", "head"),
            P("dp", "seq", "head"),
            P("head", "seq"),
        ),
        check_vma=False,
    )
```
